32 devices in a mesh: dp: 2 (over core), tensor: 16 (over z, y, x).
Axes of the slice: x: 2, y: 2, z: 4, core: 2. Of those that a mesh axis runs over, the one named last changes fastest.
Arguments:
- hidden: bfloat16 [512, 4096], P(('dp', 'tensor')), parts along dimension 0
- norm_gain: float32 [4096], replicated, may hold values from 0.3 to 3
- head_weight: bfloat16 [64128, 4096], P(('dp', 'tensor')), parts along dimension 0
- targets: int32 [512], P(('dp', 'tensor')), parts along dimension 0, may hold values from 0 to 32063
- lengths: int32 [24], P('dp'), parts along dimension 0, may hold values from 1 to 64, as said below
- offsets: int32 [24], P('dp'), parts along dimension 0, may hold values from 0 to 255, as said below
- loss_mask: int32 [512], P(('dp', 'tensor')), parts along dimension 0, may hold values from 0 to 1, as said below
Outputs:
- token_logprob: float32 [512], P(('dp', 'tensor')), parts along dimension 0
- token_entropy: float32 [512], P(('dp', 'tensor')), parts along dimension 0
- sequence_score: float32 [24], P('dp'), parts along dimension 0
The draws below stay inside these ranges and needn't reach their ends.
There are 2 independent parts, one for each index of `dp`. The reference program is written for one: setup_inputs(seed, part) draws one part's arguments, and reference() takes and returns one part's arrays. A program takes and returns all parts, laid end to end along the dimension named above; an argument that names none is the same for every part. Nothing has to cross between parts.
Inputs may be any that keep to these rules, and one draw needn't show every extreme that they name: `lengths`: responses lie in order and do not intersection within the 256 rows; one has length exactly 64. offsets[k] + lengths[k] <= offsets[k+1], and the last response ends within the pack. `loss_mask`: ones only inside responses; the 16 rows of one index of tensor hold at most 10 ones, exactly 10 on some index.
All inputs are finite; a program needn't handle non-finite values.
Results may differ from the reference program's by a relative error of at most 0.0065.
The reference program's roundings to bfloat16 on the way (of `normed`) count: a program that leaves them out, or rounds other values in their place, can miss the bound.
Values may be sent and summed in bfloat16 or wider, within the bound.
A program may use at most 128 MiB of HBM per device.

```python
import math
import jax
import jax.numpy as jnp
import numpy as np
from jax import lax

D = 4096
VOCAB_DEV = 2004
TOK_DEV = 16
SEQS = 12
LIVE_DEV = 10
TOKENS = 256
VOCAB = 32064
MAXLEN = 64
N_TENSOR = 16


def draw_hidden(key, part):
    noise_key = jax.random.fold_in(key, 11)
    row_values = jax.random.normal(noise_key, (TOKENS, D), jnp.float32)
    return row_values.astype(jnp.bfloat16)


def draw_head_weight(key, part):
    base_rows = jax.random.normal(jax.random.fold_in(key, 21), (VOCAB, D), jnp.float32) * (3.0 / math.sqrt(D))
    scale_key = jax.random.fold_in(key, 22)
    row_scale = jnp.exp(jax.random.uniform(scale_key, (VOCAB, 1), jnp.float32, math.log(0.5), math.log(2.0)))
    row_values = base_rows * row_scale
    return row_values.astype(jnp.bfloat16)


def draw_layout(key):
    short_lengths = jax.random.randint(jax.random.fold_in(key, 31), (SEQS,), 1, MAXLEN // 4 + 1)
    longest = jax.random.randint(jax.random.fold_in(key, 32), (), 0, SEQS)
    seq_index = jnp.arange(SEQS, dtype=jnp.int32)
    seq_lengths = jnp.where(seq_index == longest, MAXLEN, short_lengths).astype(jnp.int32)
    slack = TOKENS - jnp.sum(seq_lengths)
    shares = jax.random.randint(jax.random.fold_in(key, 33), (SEQS,), 0, 8)
    gap_sizes = slack * shares // (jnp.sum(shares) + 1)
    seq_offsets = (jnp.cumsum(gap_sizes) + jnp.cumsum(seq_lengths) - seq_lengths).astype(jnp.int32)
    positions = jnp.arange(TOKENS, dtype=jnp.int32)
    inside = (positions[None, :] >= seq_offsets[:, None]) & (positions[None, :] < (seq_offsets + seq_lengths)[:, None])
    covered = jnp.any(inside, axis=0)
    in_long = jnp.any(inside & (seq_index == longest)[:, None], axis=0)
    tool_rows = jax.random.randint(jax.random.fold_in(key, 34), (TOKENS,), 0, 8) == 0
    scored = covered & (in_long | jnp.logical_not(tool_rows))
    block_rows = scored.astype(jnp.int32).reshape(TOKENS // TOK_DEV, TOK_DEV)
    live_rank = jnp.cumsum(block_rows, axis=1)
    capped = (block_rows == 1) & (live_rank <= LIVE_DEV)
    return (seq_lengths, seq_offsets, capped.reshape(TOKENS).astype(jnp.int32))


def draw_lengths(key, part):
    return draw_layout(key)[0]


def draw_offsets(key, part):
    return draw_layout(key)[1]


def draw_loss_mask(key, part):
    return draw_layout(key)[2]


def plant(values, key, least, top_value):
    dims = values.shape
    index_at = [jax.random.randint(jax.random.fold_in(key, axis), (), 0, dims[axis]) for axis in range(len(dims))]
    values = values.at[tuple(index_at)].set(least)
    longest = dims.index(max(dims))
    index_at[longest] = (index_at[longest] + 1) % dims[longest]
    return values.at[tuple(index_at)].set(top_value)


def rank_bounds(count, skew):
    loads = [(1 << 20) // math.isqrt(grade ** skew) + 1 for grade in range(1, count + 1)]
    deviation = 1 + sum(loads) // (1 << 30)
    return np.cumsum(np.array([max(1, weight // deviation) for weight in loads]))


def ranked(rng, extent, count, lean):
    listing = rank_bounds(count, lean)
    lot = jax.random.randint(jax.random.fold_in(rng, 1), extent, 0, int(listing[count - 1]))
    rank = jnp.searchsorted(jnp.asarray(listing, jnp.int32), lot, side="right")
    return jax.random.permutation(jax.random.fold_in(rng, 2), count)[rank].astype(jnp.int32)


def setup_inputs(seed: int = 0, part: int = 0) -> dict:
    key_of = jax.random.split(jax.random.key(seed), 8)
    part_splits = jax.random.split(jax.random.fold_in(key_of[7], part), 8)
    return {
        "hidden": draw_hidden(jax.random.fold_in(jax.random.fold_in(key_of[7], part), 71), part),
        "norm_gain": jnp.clip(jnp.exp(jax.random.uniform(key_of[1], (D,), jnp.float32, math.log(0.3), math.log(3.0))), 0.3, 3.0),
        "head_weight": draw_head_weight(jax.random.fold_in(jax.random.fold_in(key_of[7], part), 71), part),
        "targets": plant(ranked(part_splits[3], (TOKENS,), VOCAB, 2), jax.random.fold_in(part_splits[3], 3), 0, VOCAB - 1).astype(jnp.int32),
        "lengths": draw_lengths(jax.random.fold_in(jax.random.fold_in(key_of[7], part), 71), part),
        "offsets": draw_offsets(jax.random.fold_in(jax.random.fold_in(key_of[7], part), 71), part),
        "loss_mask": draw_loss_mask(jax.random.fold_in(jax.random.fold_in(key_of[7], part), 71), part),
    }


epsilon = 1e-05

def combine_stats(earlier, later):
    peak_one, sum_one, spread_one, picked_one = earlier
    peak_two, sum_two, spread_two, picked_two = later
    new_peak = jnp.maximum(peak_one, peak_two)
    weight_early = jnp.exp(peak_one - new_peak)
    weight_late = jnp.exp(peak_two - new_peak)
    new_sum = weight_early * sum_one + weight_late * sum_two
    new_spread = weight_early * (spread_one + (peak_one - new_peak) * sum_one) + weight_late * (spread_two + (peak_two - new_peak) * sum_two)
    return (new_peak, new_sum, new_spread, picked_one + picked_two)

def reference(hidden, norm_gain, head_weight, targets, lengths, offsets, loss_mask):
    values = hidden.astype(jnp.float32)
    meansq = lax.optimization_barrier(jnp.mean(values * values, axis=1, keepdims=True))
    normed = (values * lax.rsqrt(meansq + epsilon) * norm_gain[None, :]).astype(jnp.bfloat16)
    head_blocks = head_weight.reshape(N_TENSOR, VOCAB_DEV, D)

    def vocab_step(running, inputs):
        shard_index, head_block = inputs
        scores = jnp.dot(normed, head_block.T, preferred_element_type=jnp.float32)
        row_peak = lax.optimization_barrier(jnp.max(scores, axis=1))
        centred = scores - row_peak[:, None]
        expo = jnp.exp(centred)
        row_sum = lax.optimization_barrier(jnp.sum(expo, axis=1))
        row_spread = lax.optimization_barrier(jnp.sum(expo * centred, axis=1))
        column = shard_index * VOCAB_DEV + lax.broadcasted_iota(jnp.int32, scores.shape, 1)
        picked = lax.optimization_barrier(jnp.sum(jnp.where(column == targets[:, None], scores, 0.0), axis=1))
        return (combine_stats(running, (row_peak, row_sum, row_spread, picked)), None)
    start_state = (jnp.full((TOKENS,), -1e+30, jnp.float32), jnp.zeros((TOKENS,), jnp.float32), jnp.zeros((TOKENS,), jnp.float32), jnp.zeros((TOKENS,), jnp.float32))
    final_state, unused = lax.scan(vocab_step, start_state, (jnp.arange(N_TENSOR, dtype=jnp.int32), head_blocks))
    row_peak, sum_exp, spread, target_logit = final_state
    mask_float = loss_mask.astype(jnp.float32)
    log_total = jnp.log(sum_exp)
    token_logprob = (target_logit - row_peak - log_total) * mask_float
    token_entropy = (log_total - spread / sum_exp) * mask_float
    positions = jnp.arange(TOKENS, dtype=jnp.int32)
    inside = (positions[None, :] >= offsets[:, None]) & (positions[None, :] < (offsets + lengths)[:, None])
    sequence_score = lax.optimization_barrier(jnp.sum(jnp.where(inside, token_logprob[None, :], 0.0), axis=1)) / lengths.astype(jnp.float32)
    return (token_logprob, token_entropy, sequence_score)
```

```python
import functools

import jax
import jax.numpy as jnp
from jax import lax
from jax.experimental import pallas as pl
from jax.experimental.pallas import tpu as pltpu
from jax.sharding import PartitionSpec as P

epsilon = 1e-05
LIVE = 10
MAIN = 8
REST = LIVE - MAIN
TOK = 16
CHUNK = 1024
HALF = CHUNK // 2
PIECE = CHUNK // 8
WIDE = HALF + PIECE
GROUP = 16
MESH = pl.DeviceIdType.MESH


def grid_dims(n):
    for dims in ((4, 2, 2), (4, 4, 4)):
        if dims[0] * dims[1] * dims[2] == n:
            return dims
    return (1, 1, n)


def iota(shape, dim):
    return lax.broadcasted_iota(jnp.int32, shape, dim)


def kernel(
    n,
    targets_ref,
    lengths_ref,
    offsets_ref,
    mask_ref,
    hidden_ref,
    gain_ref,
    weight_ref,
    logprob_ref,
    entropy_ref,
    score_ref,
    head,
    blocks,
    perms,
    rows,
    scores,
    meta,
    stats,
    head_sem,
    send_sem,
    recv_sem,
    meta_send,
    meta_recv,
    stat_send,
    stat_recv,
):
    vocab = weight_ref.shape[0]
    own_rows, width = hidden_ref.shape
    seqs = lengths_ref.shape[0]
    chunks = width // CHUNK
    cols = rows.shape[0]
    na, nb, nc = grid_dims(n)
    me = lax.axis_index("tensor")
    a = me // (nb * nc)
    b = (me // nc) % nb
    c = me % nc

    def at(i, j, k):
        return ((a + i) % na) * (nb * nc) + ((b + j) % nb) * nc + (c + k) % nc

    def head_copy(ch):
        return pltpu.make_async_copy(
            weight_ref.at[:, pl.ds(ch * CHUNK, CHUNK)], head.at[ch], head_sem.at[ch]
        )

    barrier = pltpu.get_barrier_semaphore()

    @pl.loop(1, n)
    def _(p):
        pl.semaphore_signal(
            barrier, inc=1, device_id={"tensor": (me + p) % n}, device_id_type=MESH
        )

    for ch in range(chunks):
        head_copy(ch).start()

    values = hidden_ref[...].astype(jnp.float32)
    meansq = jnp.mean(values * values, axis=1, keepdims=True)
    normed = (values * lax.rsqrt(meansq + epsilon) * gain_ref[...][None, :]).astype(jnp.bfloat16)

    sub = iota((TOK, own_rows), 0)
    lane = iota((TOK, own_rows), 1)
    column = iota((1, cols), 1)
    in_main = column < n * MAIN
    owner = jnp.where(in_main, column // MAIN, (column - n * MAIN) // REST)
    rank_at = jnp.where(in_main, column % MAIN, MAIN + (column - n * MAIN) % REST)
    rank_at = jnp.where(owner == me, rank_at, -1)
    rank_of = jnp.full((TOK, own_rows), -1, jnp.int32)
    ids = jnp.zeros((1, cols), jnp.int32)
    places = jnp.zeros((1, cols), jnp.int32)
    count = jnp.int32(0)
    for i in range(own_rows):
        live = mask_ref[i]
        rank = jnp.where(live == 1, count, -2)
        count = count + live
        rank_of = jnp.where(lane == i, rank, rank_of)
        ids = jnp.where(rank_at == rank, targets_ref[i], ids)
        places = jnp.where(rank_at == rank, me * own_rows + (i + 1), places)
    meta[me, 0:1, :] = ids
    meta[me, 1:2, :] = places

    def choice(begin, first, amount):
        hit = (sub >= begin) & (sub < begin + amount) & (rank_of == sub - begin + first)
        return jnp.where(hit, 1.0, 0.0).astype(jnp.bfloat16)

    def dot(x, y):
        return jnp.dot(x, y, preferred_element_type=jnp.float32)

    halves = [choice(h * MAIN, 0, MAIN) for h in range(2)]
    pieces = [choice(e * REST, MAIN, REST) for e in range(8)]
    for ch in range(chunks):
        base = ch * CHUNK
        packed = sum(
            dot(halves[h], normed[:, base + h * HALF : base + (h + 1) * HALF]) for h in range(2)
        )
        blocks[ch, me, :, 0:HALF] = packed.astype(jnp.bfloat16)
        packed = sum(
            dot(pieces[e], normed[:, base + e * PIECE : base + (e + 1) * PIECE]) for e in range(8)
        )
        blocks[ch, me, :, HALF:WIDE] = packed.astype(jnp.bfloat16)

    pl.semaphore_wait(barrier, n - 1)

    slots = [0] * chunks

    def remote(ch, src, slot, peer):
        return pltpu.make_async_remote_copy(
            src_ref=blocks.at[ch, src],
            dst_ref=blocks.at[ch, src],
            send_sem=send_sem.at[ch, slot],
            recv_sem=recv_sem.at[ch, src],
            device_id={"tensor": peer},
            device_id_type=MESH,
        )

    def send(ch, src, peer):
        remote(ch, src, slots[ch], peer).start()
        slots[ch] += 1

    def arrive(ch, src):
        remote(ch, src, 0, (me + 1) % n).wait_recv()

    def to_b(ch, src):
        for j in range(1, nb):
            send(ch, src, at(0, j, 0))

    def to_c(ch, src):
        for k in range(1, nc):
            send(ch, src, at(0, 0, k))

    def along_a(ch):
        for i in range(1, na):
            send(ch, me, at(i, 0, 0))

    def own(ch):
        to_b(ch, me)
        to_c(ch, me)

    def column_on(ch):
        for i in range(1, na):
            src = at(i, 0, 0)
            arrive(ch, src)
            to_b(ch, src)
            to_c(ch, src)

    early = (na + 1) // 2

    def across(ch):
        for i in range(na):
            if i < early:
                for j in range(1, nb):
                    arrive(ch, at(i, j, 0))
                    to_c(ch, at(i, j, 0))
            else:
                for k in range(1, nc):
                    arrive(ch, at(i, 0, k))
                    to_b(ch, at(i, 0, k))

    def settle(ch):
        for i in range(na):
            if i < early:
                for k in range(1, nc):
                    arrive(ch, at(i, 0, k))
            else:
                for j in range(1, nb):
                    arrive(ch, at(i, j, 0))
            for j in range(1, nb):
                for k in range(1, nc):
                    arrive(ch, at(i, j, k))

    def meta_copy(p):
        return pltpu.make_async_remote_copy(
            src_ref=meta.at[me],
            dst_ref=meta.at[me],
            send_sem=meta_send.at[p],
            recv_sem=meta_recv.at[me],
            device_id={"tensor": (me + p) % n},
            device_id_type=MESH,
        )

    def stat_copy(p):
        return pltpu.make_async_remote_copy(
            src_ref=stats.at[me],
            dst_ref=stats.at[me],
            send_sem=stat_send.at[p],
            recv_sem=stat_recv.at[me],
            device_id={"tensor": (me + p) % n},
            device_id_type=MESH,
        )

    along_a(0)
    own(0)
    for ch in range(1, chunks):
        along_a(ch)
        if ch == 1:
            own(1)

    @pl.loop(1, n)
    def _(p):
        meta_copy(p).start()

    size = GROUP * TOK
    out_row = iota((size, size), 0)
    in_row = iota((size, size), 1)
    span = GROUP * MAIN
    source = (out_row % span) // MAIN * TOK + out_row // span * MAIN + out_row % MAIN
    perms[0] = jnp.where(in_row == source, 1.0, 0.0).astype(jnp.bfloat16)
    span = GROUP * REST
    source = (out_row % span) // REST * TOK + out_row // span * REST + out_row % REST
    perms[1] = jnp.where(in_row == source, 1.0, 0.0).astype(jnp.bfloat16)
    used = n * LIVE
    if used < cols:
        rows[used:cols, :] = jnp.zeros((cols - used, CHUNK), jnp.bfloat16)

    def unpack(ch):
        for g in range(n // GROUP):
            main = blocks[ch, g * GROUP : (g + 1) * GROUP, :, 0:HALF].reshape(size, HALF)
            main = dot(perms[0], main).astype(jnp.bfloat16)
            span = GROUP * MAIN
            for h in range(2):
                rows[g * span : (g + 1) * span, h * HALF : (h + 1) * HALF] = main[
                    h * span : (h + 1) * span
                ]
            rest = blocks[ch, g * GROUP : (g + 1) * GROUP, :, HALF:WIDE].reshape(size, PIECE)
            rest = dot(perms[1], rest).astype(jnp.bfloat16)
            span = GROUP * REST
            top = n * MAIN + g * span
            for e in range(8):
                rows[top : top + span, e * PIECE : (e + 1) * PIECE] = rest[
                    e * span : (e + 1) * span
                ]

    step = 256
    full = vocab // step

    def tiles(body, carry):
        carry = lax.fori_loop(
            0, full, lambda t, v: body(pl.multiple_of(t * step, step), step, v), carry
        )
        if vocab % step:
            carry = body(full * step, vocab % step, carry)
        return carry

    def partial(ch):
        head_copy(ch).wait()

        def body(begin, amount, peak):
            tile = lax.dot_general(
                head[ch, pl.ds(begin, amount), :],
                rows[...],
                (((1,), (1,)), ((), ())),
                preferred_element_type=jnp.float32,
            )
            if ch > 0:
                tile = tile + scores[pl.ds(begin, amount), :]
            scores[pl.ds(begin, amount), :] = tile
            if ch == chunks - 1:
                peak = jnp.maximum(peak, jnp.max(tile, axis=0, keepdims=True))
            return peak

        return tiles(body, jnp.full((1, cols), -jnp.inf, jnp.float32))

    column_on(0)
    if chunks > 1:
        column_on(1)
    across(0)
    if chunks > 2:
        own(2)
    for ch in range(chunks):
        if ch + 2 < chunks:
            column_on(ch + 2)
        if ch + 1 < chunks:
            across(ch + 1)
        if ch + 3 < chunks:
            own(ch + 3)
        settle(ch)
        unpack(ch)
        peak = partial(ch)

    @pl.loop(1, n)
    def _(p):
        other = (me + p) % n
        pltpu.make_async_remote_copy(
            src_ref=meta.at[other],
            dst_ref=meta.at[other],
            send_sem=meta_send.at[p],
            recv_sem=meta_recv.at[other],
            device_id={"tensor": other},
            device_id_type=MESH,
        ).wait_recv()

    ids = sum(meta[s, 0:1, :] for s in range(n))
    places = sum(meta[s, 1:2, :] for s in range(n)) - 1
    local_ids = ids - me * vocab

    def collect(begin, amount, carry):
        row_sum, spread, picked = carry
        tile = scores[pl.ds(begin, amount), :]
        centred = tile - peak
        expo = jnp.exp(centred)
        entry = begin + iota(tile.shape, 0)
        row_sum = row_sum + jnp.sum(expo, axis=0, keepdims=True)
        spread = spread + jnp.sum(expo * centred, axis=0, keepdims=True)
        picked = picked + jnp.sum(
            jnp.where(entry == local_ids, tile, 0.0), axis=0, keepdims=True
        )
        return row_sum, spread, picked

    nothing = jnp.zeros((1, cols), jnp.float32)
    row_sum, spread, picked = tiles(collect, (nothing, nothing, nothing))
    stats[me, 0:1, :] = peak
    stats[me, 1:2, :] = row_sum
    stats[me, 2:3, :] = spread
    stats[me, 3:4, :] = picked

    @pl.loop(1, n)
    def _(p):
        stat_copy(p).start()

    tall = iota((own_rows, cols), 0)
    mine = places == me * own_rows + tall
    kept = iota((seqs, 1), 0)
    first = jnp.zeros((seqs, 1), jnp.int32)
    length = jnp.ones((seqs, 1), jnp.int32)
    for k in range(seqs):
        first = jnp.where(kept == k, offsets_ref[k], first)
        length = jnp.where(kept == k, lengths_ref[k], length)
    inside = (places >= first) & (places < first + length)

    @pl.loop(1, n)
    def _(p):
        other = (me + p) % n
        pltpu.make_async_remote_copy(
            src_ref=stats.at[other],
            dst_ref=stats.at[other],
            send_sem=stat_send.at[p],
            recv_sem=stat_recv.at[other],
            device_id={"tensor": other},
            device_id_type=MESH,
        ).wait_recv()

    top = functools.reduce(jnp.maximum, [stats[s, 0:1, :] for s in range(n)])
    sum_exp, spread, picked = nothing, nothing, nothing
    for s in range(n):
        shift = stats[s, 0:1, :] - top
        factor = jnp.exp(shift)
        part = stats[s, 1:2, :]
        sum_exp = sum_exp + factor * part
        spread = spread + factor * (stats[s, 2:3, :] + shift * part)
        picked = picked + stats[s, 3:4, :]
    log_total = jnp.log(sum_exp)
    logprob = picked - top - log_total
    entropy = log_total - spread / sum_exp

    def lay(col):
        amount = col.shape[0]
        square = iota((amount, amount), 0) == iota((amount, amount), 1)
        return jnp.sum(jnp.where(square, col, 0.0), axis=0, keepdims=True)

    def total(where, value):
        return jnp.sum(jnp.where(where, value, 0.0), axis=1, keepdims=True)

    logprob_ref[...] = lay(total(mine, logprob))
    entropy_ref[...] = lay(total(mine, entropy))
    score_ref[...] = lay(total(inside, logprob) / length.astype(jnp.float32))

    for ch in range(chunks):
        for slot in range(slots[ch]):
            remote(ch, me, slot, (me + 1) % n).wait_send()

    @pl.loop(1, n)
    def _(p):
        meta_copy(p).wait_send()
        stat_copy(p).wait_send()


def local(n, hidden, norm_gain, head_weight, targets, lengths, offsets, loss_mask):
    own_rows, width = hidden.shape
    vocab = head_weight.shape[0]
    seqs = lengths.shape[0]
    chunks = width // CHUNK
    cols = -(-n * LIVE // 128) * 128
    smem = pl.BlockSpec(memory_space=pltpu.SMEM)
    vmem = pl.BlockSpec(memory_space=pltpu.VMEM)
    dma = pltpu.SemaphoreType.DMA
    logprob, entropy, score = pl.pallas_call(
        functools.partial(kernel, n),
        out_shape=(
            jax.ShapeDtypeStruct((1, own_rows), jnp.float32),
            jax.ShapeDtypeStruct((1, own_rows), jnp.float32),
            jax.ShapeDtypeStruct((1, seqs), jnp.float32),
        ),
        in_specs=[smem] * 4 + [vmem, vmem, pl.BlockSpec(memory_space=pl.ANY)],
        out_specs=(vmem, vmem, vmem),
        scratch_shapes=[
            pltpu.VMEM((chunks, vocab, CHUNK), jnp.bfloat16),
            pltpu.VMEM((chunks, n, TOK, WIDE), jnp.bfloat16),
            pltpu.VMEM((2, GROUP * TOK, GROUP * TOK), jnp.bfloat16),
            pltpu.VMEM((cols, CHUNK), jnp.bfloat16),
            pltpu.VMEM((vocab, cols), jnp.float32),
            pltpu.VMEM((n, 2, cols), jnp.int32),
            pltpu.VMEM((n, 4, cols), jnp.float32),
            dma((chunks,)),
            dma((chunks, n)),
            dma((chunks, n)),
            dma((n,)),
            dma((n,)),
            dma((n,)),
            dma((n,)),
        ],
        compiler_params=pltpu.CompilerParams(
            collective_id=0, has_side_effects=True, vmem_limit_bytes=48 * 2**20
        ),
        cost_estimate=pl.CostEstimate(
            flops=2 * vocab * width * n * LIVE,
            bytes_accessed=2 * vocab * width,
            transcendentals=vocab * n * LIVE,
        ),
        name="head_stats",
    )(targets, lengths, offsets, loss_mask, hidden, norm_gain, head_weight)
    return logprob.reshape(own_rows), entropy.reshape(own_rows), score.reshape(seqs)


def solution(mesh):
    return jax.shard_map(
        functools.partial(local, mesh.shape["tensor"]),
        mesh=mesh,
        in_specs=(
            P(("dp", "tensor"), None),
            P(),
            P(("dp", "tensor"), None),
            P(("dp", "tensor")),
            P("dp"),
            P("dp"),
            P(("dp", "tensor")),
        ),
        out_specs=(P(("dp", "tensor")), P(("dp", "tensor")), P("dp")),
        check_vma=False,
    )
```

```python
import functools

import jax
import jax.numpy as jnp
from jax import lax
from jax.experimental import pallas as pl
from jax.experimental.pallas import tpu as pltpu
from jax.sharding import PartitionSpec as P

epsilon = 1e-05
LIVE = 10
MAIN = 8
REST = LIVE - MAIN
TOK = 16
CHUNK = 1024
HALF = CHUNK // 2
PIECE = CHUNK // 8
WIDE = HALF + PIECE
GROUP = 16
MESH = pl.DeviceIdType.MESH


def grid_dims(n):
    for dims in ((4, 2, 2), (4, 4, 4)):
        if dims[0] * dims[1] * dims[2] == n:
            return dims
    return (1, 1, n)


def iota(shape, dim):
    return lax.broadcasted_iota(jnp.int32, shape, dim)


def kernel(
    n,
    targets_hbm,
    lengths_hbm,
    offsets_hbm,
    mask_hbm,
    hidden_hbm,
    gain_hbm,
    weight_ref,
    logprob_ref,
    entropy_ref,
    score_ref,
    targets_ref,
    lengths_ref,
    offsets_ref,
    mask_ref,
    hidden_ref,
    gain_ref,
    head,
    blocks,
    main_perm,
    rest_perm,
    rows,
    scores,
    meta,
    stats,
    in_sem,
    head_sem,
    send_sem,
    recv_sem,
    meta_send,
    meta_recv,
    stat_send,
    stat_recv,
):
    vocab = weight_ref.shape[0]
    own_rows, width = hidden_ref.shape
    seqs = lengths_ref.shape[0]
    chunks = width // CHUNK
    cols = rows.shape[1]
    na, nb, nc = grid_dims(n)
    me = lax.axis_index("tensor")
    a = me // (nb * nc)
    b = (me // nc) % nb
    c = me % nc

    def at(i, j, k):
        return ((a + i) % na) * (nb * nc) + ((b + j) % nb) * nc + (c + k) % nc

    def head_copy(ch):
        return pltpu.make_async_copy(
            weight_ref.at[:, pl.ds(ch * CHUNK, CHUNK)], head.at[ch], head_sem.at[ch]
        )

    barrier = pltpu.get_barrier_semaphore()

    @pl.loop(1, n)
    def _(p):
        pl.semaphore_signal(
            barrier, inc=1, device_id={"tensor": (me + p) % n}, device_id_type=MESH
        )

    small = [
        pltpu.make_async_copy(there, here, in_sem.at[i])
        for i, (there, here) in enumerate(
            (
                (hidden_hbm, hidden_ref),
                (gain_hbm, gain_ref),
                (mask_hbm, mask_ref),
                (targets_hbm, targets_ref),
                (lengths_hbm, lengths_ref),
                (offsets_hbm, offsets_ref),
            )
        )
    ]
    for copy in small:
        copy.start()
    for ch in range(chunks):
        head_copy(ch).start()
    for copy in small:
        copy.wait()

    values = hidden_ref[...].astype(jnp.float32)
    meansq = jnp.mean(values * values, axis=1, keepdims=True)
    normed = (values * lax.rsqrt(meansq + epsilon) * gain_ref[...][None, :]).astype(jnp.bfloat16)

    sub = iota((TOK, own_rows), 0)
    lane = iota((TOK, own_rows), 1)
    rank_of = jnp.full((TOK, own_rows), -1, jnp.int32)
    ranks = []
    count = jnp.int32(0)
    for i in range(own_rows):
        live = mask_ref[i]
        ranks.append(jnp.where(live == 1, count, -2))
        count = count + live
        rank_of = jnp.where(lane == i, ranks[i], rank_of)

    def choice(begin, first, amount):
        hit = (sub >= begin) & (sub < begin + amount) & (rank_of == sub - begin + first)
        return jnp.where(hit, 1.0, 0.0).astype(jnp.bfloat16)

    def dot(x, y):
        return jnp.dot(x, y, preferred_element_type=jnp.float32)

    halves = [choice(h * MAIN, 0, MAIN) for h in range(2)]
    pieces = [choice(e * REST, MAIN, REST) for e in range(8)]

    def pack(ch):
        base = ch * CHUNK
        packed = sum(
            dot(halves[h], normed[:, base + h * HALF : base + (h + 1) * HALF]) for h in range(2)
        )
        blocks[ch, me, :, 0:HALF] = packed.astype(jnp.bfloat16)
        packed = sum(
            dot(pieces[e], normed[:, base + e * PIECE : base + (e + 1) * PIECE]) for e in range(8)
        )
        blocks[ch, me, :, HALF:WIDE] = packed.astype(jnp.bfloat16)

    slots = [0] * chunks

    def remote(ch, src, slot, peer):
        return pltpu.make_async_remote_copy(
            src_ref=blocks.at[ch, src],
            dst_ref=blocks.at[ch, src],
            send_sem=send_sem.at[ch, slot],
            recv_sem=recv_sem.at[ch, src],
            device_id={"tensor": peer},
            device_id_type=MESH,
        )

    def send(ch, src, peer):
        remote(ch, src, slots[ch], peer).start()
        slots[ch] += 1

    def arrive(ch, src):
        remote(ch, src, 0, (me + 1) % n).wait_recv()

    def to_b(ch, src):
        for j in range(1, nb):
            send(ch, src, at(0, j, 0))

    def to_c(ch, src):
        for k in range(1, nc):
            send(ch, src, at(0, 0, k))

    def along_a(ch):
        for i in range(1, na):
            send(ch, me, at(i, 0, 0))

    def own(ch):
        to_b(ch, me)
        to_c(ch, me)

    def column_on(ch):
        for i in range(1, na):
            src = at(i, 0, 0)
            arrive(ch, src)
            to_b(ch, src)
            to_c(ch, src)

    early = (na + 1) // 2

    def across(ch):
        for i in range(na):
            if i < early:
                for j in range(1, nb):
                    arrive(ch, at(i, j, 0))
                    to_c(ch, at(i, j, 0))
            else:
                for k in range(1, nc):
                    arrive(ch, at(i, 0, k))
                    to_b(ch, at(i, 0, k))

    def settle(ch):
        for i in range(na):
            if i < early:
                for k in range(1, nc):
                    arrive(ch, at(i, 0, k))
            else:
                for j in range(1, nb):
                    arrive(ch, at(i, j, 0))
            for j in range(1, nb):
                for k in range(1, nc):
                    arrive(ch, at(i, j, k))

    def meta_copy(p):
        return pltpu.make_async_remote_copy(
            src_ref=meta.at[me],
            dst_ref=meta.at[me],
            send_sem=meta_send.at[p],
            recv_sem=meta_recv.at[me],
            device_id={"tensor": (me + p) % n},
            device_id_type=MESH,
        )

    def stat_copy(p):
        return pltpu.make_async_remote_copy(
            src_ref=stats.at[me],
            dst_ref=stats.at[me],
            send_sem=stat_send.at[p],
            recv_sem=stat_recv.at[me],
            device_id={"tensor": (me + p) % n},
            device_id_type=MESH,
        )

    pack(0)
    pl.semaphore_wait(barrier, n - 1)
    along_a(0)
    own(0)
    for ch in range(1, chunks):
        pack(ch)
        along_a(ch)
        if ch == 1:
            own(1)

    column = iota((1, cols), 1)
    in_main = column < n * MAIN
    owner = jnp.where(in_main, column // MAIN, (column - n * MAIN) // REST)
    rank_at = jnp.where(in_main, column % MAIN, MAIN + (column - n * MAIN) % REST)
    rank_at = jnp.where(owner == me, rank_at, -1)
    ids = jnp.zeros((1, cols), jnp.int32)
    places = jnp.zeros((1, cols), jnp.int32)
    for i in range(own_rows):
        ids = jnp.where(rank_at == ranks[i], targets_ref[i], ids)
        places = jnp.where(rank_at == ranks[i], me * own_rows + (i + 1), places)
    meta[me, 0:1, :] = ids
    meta[me, 1:2, :] = places

    @pl.loop(1, n)
    def _(p):
        meta_copy(p).start()

    groups = n // GROUP
    size = GROUP * TOK
    in_row = iota((size, size), 0)
    out_col = iota((size, size), 1)
    span = GROUP * MAIN
    source = (out_col % span) // MAIN * TOK + out_col // span * MAIN + out_col % MAIN
    main_perm[...] = jnp.where(in_row == source, 1.0, 0.0).astype(jnp.bfloat16)
    tail = cols - n * MAIN
    in_row = iota((size, tail), 0)
    for g in range(groups):
        out_col = iota((size, tail), 1) - g * GROUP * REST
        valid = (out_col >= 0) & (out_col < GROUP * REST)
        for e in range(8):
            source = out_col // REST * TOK + e * REST + out_col % REST
            rest_perm[g * 8 + e] = jnp.where(valid & (in_row == source), 1.0, 0.0).astype(
                jnp.bfloat16
            )

    def turned(x, y):
        return lax.dot_general(
            x, y, (((0,), (0,)), ((), ())), preferred_element_type=jnp.float32
        )

    def unpack(ch):
        span = GROUP * MAIN
        tops = [
            blocks[ch, g * GROUP : (g + 1) * GROUP, :, 0:HALF].reshape(size, HALF)
            for g in range(groups)
        ]
        rests = [
            blocks[ch, g * GROUP : (g + 1) * GROUP, :, HALF:WIDE].reshape(size, PIECE)
            for g in range(groups)
        ]
        for g in range(groups):
            main = turned(tops[g], main_perm[...]).astype(jnp.bfloat16)
            for h in range(2):
                rows[h * HALF : (h + 1) * HALF, g * span : (g + 1) * span] = main[
                    :, h * span : (h + 1) * span
                ]
        for e in range(8):
            rest = sum(turned(rests[g], rest_perm[g * 8 + e]) for g in range(groups))
            rows[e * PIECE : (e + 1) * PIECE, n * MAIN : cols] = rest.astype(jnp.bfloat16)

    def tiles(extent, step, body, carry):
        full = extent // step
        carry = lax.fori_loop(
            0, full, lambda t, v: body(pl.multiple_of(t * step, step), step, v), carry
        )
        if extent % step:
            carry = body(full * step, extent % step, carry)
        return carry

    def partial(ch):
        head_copy(ch).wait()

        def body(begin, amount, peak):
            tile = dot(head[ch, pl.ds(begin, amount), :], rows[...])
            if ch > 0:
                tile = tile + scores[pl.ds(begin, amount), :]
            scores[pl.ds(begin, amount), :] = tile
            if ch == chunks - 1:
                peak = jnp.maximum(peak, jnp.max(tile, axis=0, keepdims=True))
            return peak

        return tiles(vocab, 512, body, jnp.full((1, cols), -jnp.inf, jnp.float32))

    padded = scores.shape[0]
    if padded > vocab:
        scores[vocab:padded, :] = jnp.full((padded - vocab, cols), -1e30, jnp.float32)

    column_on(0)
    if chunks > 1:
        column_on(1)
    across(0)
    if chunks > 2:
        own(2)
    for ch in range(chunks):
        if ch + 2 < chunks:
            column_on(ch + 2)
        if ch + 1 < chunks:
            across(ch + 1)
        if ch + 3 < chunks:
            own(ch + 3)
        settle(ch)
        unpack(ch)
        peak = partial(ch)

    @pl.loop(1, n)
    def _(p):
        other = (me + p) % n
        pltpu.make_async_remote_copy(
            src_ref=meta.at[other],
            dst_ref=meta.at[other],
            send_sem=meta_send.at[p],
            recv_sem=meta_recv.at[other],
            device_id={"tensor": other},
            device_id_type=MESH,
        ).wait_recv()

    ids = sum(meta[s, 0:1, :] for s in range(n))
    places = sum(meta[s, 1:2, :] for s in range(n)) - 1
    local_ids = ids - me * vocab
    local_ids = jnp.where(local_ids < vocab, local_ids, -1)

    def collect(begin, amount, carry):
        row_sum, spread, picked = carry
        tile = scores[pl.ds(begin, amount), :]
        centred = tile - peak
        expo = jnp.exp(centred)
        entry = begin + iota(tile.shape, 0)
        given = jnp.where(entry == local_ids, tile, 0.0)

        def fold(x):
            return jnp.sum(x.reshape(amount // 8, 8, cols), axis=0)

        return row_sum + fold(expo), spread + fold(expo * centred), picked + fold(given)

    nothing = jnp.zeros((8, cols), jnp.float32)
    row_sum, spread, picked = (
        jnp.sum(x, axis=0, keepdims=True)
        for x in tiles(padded, 64, collect, (nothing, nothing, nothing))
    )
    nothing = nothing[0:1]
    stats[me, 0:1, :] = peak
    stats[me, 1:2, :] = row_sum
    stats[me, 2:3, :] = spread
    stats[me, 3:4, :] = picked

    @pl.loop(1, n)
    def _(p):
        stat_copy(p).start()

    tall = iota((own_rows, cols), 0)
    mine = places == me * own_rows + tall
    kept = iota((seqs, 1), 0)
    first = jnp.zeros((seqs, 1), jnp.int32)
    length = jnp.ones((seqs, 1), jnp.int32)
    for k in range(seqs):
        first = jnp.where(kept == k, offsets_ref[k], first)
        length = jnp.where(kept == k, lengths_ref[k], length)
    inside = (places >= first) & (places < first + length)

    @pl.loop(1, n)
    def _(p):
        other = (me + p) % n
        pltpu.make_async_remote_copy(
            src_ref=stats.at[other],
            dst_ref=stats.at[other],
            send_sem=stat_send.at[p],
            recv_sem=stat_recv.at[other],
            device_id={"tensor": other},
            device_id_type=MESH,
        ).wait_recv()

    top = functools.reduce(jnp.maximum, [stats[s, 0:1, :] for s in range(n)])
    sum_exp, spread, picked = nothing, nothing, nothing
    for s in range(n):
        shift = stats[s, 0:1, :] - top
        factor = jnp.exp(shift)
        part = stats[s, 1:2, :]
        sum_exp = sum_exp + factor * part
        spread = spread + factor * (stats[s, 2:3, :] + shift * part)
        picked = picked + stats[s, 3:4, :]
    log_total = jnp.log(sum_exp)
    logprob = picked - top - log_total
    entropy = log_total - spread / sum_exp

    def lay(col):
        amount = col.shape[0]
        square = iota((amount, amount), 0) == iota((amount, amount), 1)
        return jnp.sum(jnp.where(square, col, 0.0), axis=0, keepdims=True)

    def total(where, value):
        return jnp.sum(jnp.where(where, value, 0.0), axis=1, keepdims=True)

    logprob_ref[...] = lay(total(mine, logprob))
    entropy_ref[...] = lay(total(mine, entropy))
    score_ref[...] = lay(total(inside, logprob) / length.astype(jnp.float32))

    for ch in range(chunks):
        for slot in range(slots[ch]):
            remote(ch, me, slot, (me + 1) % n).wait_send()

    @pl.loop(1, n)
    def _(p):
        meta_copy(p).wait_send()
        stat_copy(p).wait_send()


def local(n, hidden, norm_gain, head_weight, targets, lengths, offsets, loss_mask):
    own_rows, width = hidden.shape
    vocab = head_weight.shape[0]
    seqs = lengths.shape[0]
    chunks = width // CHUNK
    cols = n * MAIN + 128
    hbm = pl.BlockSpec(memory_space=pltpu.HBM)
    vmem = pl.BlockSpec(memory_space=pltpu.VMEM)
    dma = pltpu.SemaphoreType.DMA
    logprob, entropy, score = pl.pallas_call(
        functools.partial(kernel, n),
        out_shape=(
            jax.ShapeDtypeStruct((1, own_rows), jnp.float32),
            jax.ShapeDtypeStruct((1, own_rows), jnp.float32),
            jax.ShapeDtypeStruct((1, seqs), jnp.float32),
        ),
        in_specs=[hbm] * 7,
        out_specs=(vmem, vmem, vmem),
        scratch_shapes=[
            pltpu.SMEM((own_rows,), jnp.int32),
            pltpu.SMEM((seqs,), jnp.int32),
            pltpu.SMEM((seqs,), jnp.int32),
            pltpu.SMEM((own_rows,), jnp.int32),
            pltpu.VMEM((own_rows, width), jnp.bfloat16),
            pltpu.VMEM((width,), jnp.float32),
            pltpu.VMEM((chunks, vocab, CHUNK), jnp.bfloat16),
            pltpu.VMEM((chunks, n, TOK, WIDE), jnp.bfloat16),
            pltpu.VMEM((GROUP * TOK, GROUP * TOK), jnp.bfloat16),
            pltpu.VMEM((n // GROUP * 8, GROUP * TOK, 128), jnp.bfloat16),
            pltpu.VMEM((CHUNK, cols), jnp.bfloat16),
            pltpu.VMEM((-(-vocab // 8) * 8, cols), jnp.float32),
            pltpu.VMEM((n, 2, cols), jnp.int32),
            pltpu.VMEM((n, 4, cols), jnp.float32),
            dma((6,)),
            dma((chunks,)),
            dma((chunks, n)),
            dma((chunks, n)),
            dma((n,)),
            dma((n,)),
            dma((n,)),
            dma((n,)),
        ],
        compiler_params=pltpu.CompilerParams(
            collective_id=0, has_side_effects=True, vmem_limit_bytes=64 * 2**20
        ),
        cost_estimate=pl.CostEstimate(
            flops=2 * vocab * width * n * LIVE,
            bytes_accessed=2 * vocab * width,
            transcendentals=vocab * n * LIVE,
        ),
        name="head_stats",
    )(targets, lengths, offsets, loss_mask, hidden, norm_gain, head_weight)
    return logprob.reshape(own_rows), entropy.reshape(own_rows), score.reshape(seqs)


def solution(mesh):
    return jax.shard_map(
        functools.partial(local, mesh.shape["tensor"]),
        mesh=mesh,
        in_specs=(
            P(("dp", "tensor"), None),
            P(),
            P(("dp", "tensor"), None),
            P(("dp", "tensor")),
            P("dp"),
            P("dp"),
            P(("dp", "tensor")),
        ),
        out_specs=(P(("dp", "tensor")), P(("dp", "tensor")), P("dp")),
        check_vma=False,
    )
```

```python
import functools

import jax
import jax.numpy as jnp
from jax import lax
from jax.experimental import pallas as pl
from jax.experimental.pallas import tpu as pltpu
from jax.sharding import PartitionSpec as P

epsilon = 1e-05
LIVE = 10
MAIN = 8
REST = LIVE - MAIN
TOK = 16
CHUNK = 1024
HALF = CHUNK // 2
PIECE = CHUNK // 8
WIDE = HALF + PIECE
GROUP = 16
MESH = pl.DeviceIdType.MESH


def grid_dims(n):
    for dims in ((4, 2, 2), (4, 4, 4)):
        if dims[0] * dims[1] * dims[2] == n:
            return dims
    return (1, 1, n)


def iota(shape, dim):
    return lax.broadcasted_iota(jnp.int32, shape, dim)


def kernel(
    n,
    targets_hbm,
    lengths_hbm,
    offsets_hbm,
    mask_hbm,
    hidden_hbm,
    gain_hbm,
    weight_ref,
    result_ref,
    targets_ref,
    lengths_ref,
    offsets_ref,
    mask_ref,
    hidden_ref,
    gain_ref,
    head,
    blocks,
    main_perm,
    rest_perm,
    rows,
    scores,
    meta,
    stats,
    in_sem,
    head_sem,
    send_sem,
    recv_sem,
    meta_send,
    meta_recv,
    stat_send,
    stat_recv,
):
    vocab = weight_ref.shape[0]
    own_rows, width = hidden_ref.shape
    seqs = lengths_ref.shape[0]
    chunks = width // CHUNK
    cols = rows.shape[1]
    na, nb, nc = grid_dims(n)
    me = lax.axis_index("tensor")
    a = me // (nb * nc)
    b = (me // nc) % nb
    c = me % nc

    def at(i, j, k):
        return ((a + i) % na) * (nb * nc) + ((b + j) % nb) * nc + (c + k) % nc

    def head_copy(ch):
        return pltpu.make_async_copy(
            weight_ref.at[:, pl.ds(ch * CHUNK, CHUNK)], head.at[ch], head_sem.at[ch]
        )

    barrier = pltpu.get_barrier_semaphore()

    @pl.loop(1, n)
    def _(p):
        pl.semaphore_signal(
            barrier, inc=1, device_id={"tensor": (me + p) % n}, device_id_type=MESH
        )

    small = [
        pltpu.make_async_copy(there, here, in_sem.at[i])
        for i, (there, here) in enumerate(
            (
                (hidden_hbm, hidden_ref),
                (gain_hbm, gain_ref),
                (mask_hbm, mask_ref),
                (targets_hbm, targets_ref),
                (lengths_hbm, lengths_ref),
                (offsets_hbm, offsets_ref),
            )
        )
    ]
    for copy in small:
        copy.start()
    for ch in range(chunks):
        head_copy(ch).start()
    for copy in small:
        copy.wait()

    values = hidden_ref[...].astype(jnp.float32)
    meansq = jnp.mean(values * values, axis=1, keepdims=True)
    normed = (values * lax.rsqrt(meansq + epsilon) * gain_ref[...][None, :]).astype(jnp.bfloat16)

    sub = iota((TOK, own_rows), 0)
    lane = iota((TOK, own_rows), 1)
    rank_of = jnp.full((TOK, own_rows), -1, jnp.int32)
    ranks = []
    count = jnp.int32(0)
    for i in range(own_rows):
        live = mask_ref[i]
        ranks.append(jnp.where(live == 1, count, -2))
        count = count + live
        rank_of = jnp.where(lane == i, ranks[i], rank_of)

    def choice(begin, first, amount):
        hit = (sub >= begin) & (sub < begin + amount) & (rank_of == sub - begin + first)
        return jnp.where(hit, 1.0, 0.0).astype(jnp.bfloat16)

    def dot(x, y):
        return jnp.dot(x, y, preferred_element_type=jnp.float32)

    halves = [choice(h * MAIN, 0, MAIN) for h in range(2)]
    pieces = [choice(e * REST, MAIN, REST) for e in range(8)]

    def pack(ch):
        base = ch * CHUNK
        packed = sum(
            dot(halves[h], normed[:, base + h * HALF : base + (h + 1) * HALF]) for h in range(2)
        )
        blocks[ch, me, :, 0:HALF] = packed.astype(jnp.bfloat16)
        packed = sum(
            dot(pieces[e], normed[:, base + e * PIECE : base + (e + 1) * PIECE]) for e in range(8)
        )
        blocks[ch, me, :, HALF:WIDE] = packed.astype(jnp.bfloat16)

    slots = [0] * chunks

    def remote(ch, src, slot, peer):
        return pltpu.make_async_remote_copy(
            src_ref=blocks.at[ch, src],
            dst_ref=blocks.at[ch, src],
            send_sem=send_sem.at[ch, slot],
            recv_sem=recv_sem.at[ch, src],
            device_id={"tensor": peer},
            device_id_type=MESH,
        )

    def send(ch, src, peer):
        remote(ch, src, slots[ch], peer).start()
        slots[ch] += 1

    def arrive(ch, src):
        remote(ch, src, 0, (me + 1) % n).wait_recv()

    def to_b(ch, src):
        for j in range(1, nb):
            send(ch, src, at(0, j, 0))

    def to_c(ch, src):
        for k in range(1, nc):
            send(ch, src, at(0, 0, k))

    def along_a(ch):
        for i in range(1, na):
            send(ch, me, at(i, 0, 0))

    def own(ch):
        to_b(ch, me)
        to_c(ch, me)

    def column_on(ch):
        for i in range(1, na):
            src = at(i, 0, 0)
            arrive(ch, src)
            to_b(ch, src)
            to_c(ch, src)

    early = (na + 1) // 2

    def across(ch):
        for i in range(na):
            if i < early:
                for j in range(1, nb):
                    arrive(ch, at(i, j, 0))
                    to_c(ch, at(i, j, 0))
            else:
                for k in range(1, nc):
                    arrive(ch, at(i, 0, k))
                    to_b(ch, at(i, 0, k))

    def settle(ch):
        for i in range(na):
            if i < early:
                for k in range(1, nc):
                    arrive(ch, at(i, 0, k))
            else:
                for j in range(1, nb):
                    arrive(ch, at(i, j, 0))
            for j in range(1, nb):
                for k in range(1, nc):
                    arrive(ch, at(i, j, k))

    def meta_copy(p):
        return pltpu.make_async_remote_copy(
            src_ref=meta.at[me],
            dst_ref=meta.at[me],
            send_sem=meta_send.at[p],
            recv_sem=meta_recv.at[me],
            device_id={"tensor": (me + p) % n},
            device_id_type=MESH,
        )

    def stat_copy(p):
        return pltpu.make_async_remote_copy(
            src_ref=stats.at[me],
            dst_ref=stats.at[me],
            send_sem=stat_send.at[p],
            recv_sem=stat_recv.at[me],
            device_id={"tensor": (me + p) % n},
            device_id_type=MESH,
        )

    pack(0)
    pl.semaphore_wait(barrier, n - 1)
    along_a(0)
    own(0)
    for ch in range(1, chunks):
        pack(ch)
        along_a(ch)
        own(ch)

    column = iota((1, cols), 1)
    in_main = column < n * MAIN
    owner = jnp.where(in_main, column // MAIN, (column - n * MAIN) // REST)
    rank_at = jnp.where(in_main, column % MAIN, MAIN + (column - n * MAIN) % REST)
    rank_at = jnp.where(owner == me, rank_at, -1)
    ids = jnp.zeros((1, cols), jnp.int32)
    places = jnp.zeros((1, cols), jnp.int32)
    for i in range(own_rows):
        ids = jnp.where(rank_at == ranks[i], targets_ref[i], ids)
        places = jnp.where(rank_at == ranks[i], me * own_rows + (i + 1), places)
    meta[me, 0:1, :] = ids
    meta[me, 1:2, :] = places

    @pl.loop(1, n)
    def _(p):
        meta_copy(p).start()

    column_on(0)
    if chunks > 1:
        column_on(1)

    groups = n // GROUP
    size = GROUP * TOK
    in_row = iota((size, size), 0)
    out_col = iota((size, size), 1)
    span = GROUP * MAIN
    source = (out_col % span) // MAIN * TOK + out_col // span * MAIN + out_col % MAIN
    main_perm[...] = jnp.where(in_row == source, 1.0, 0.0).astype(jnp.bfloat16)
    tail = cols - n * MAIN
    in_row = iota((size, tail), 0)
    for g in range(groups):
        out_col = iota((size, tail), 1) - g * GROUP * REST
        valid = (out_col >= 0) & (out_col < GROUP * REST)
        for e in range(8):
            source = out_col // REST * TOK + e * REST + out_col % REST
            rest_perm[g * 8 + e] = jnp.where(valid & (in_row == source), 1.0, 0.0).astype(
                jnp.bfloat16
            )

    def turned(x, y):
        return lax.dot_general(
            x, y, (((0,), (0,)), ((), ())), preferred_element_type=jnp.float32
        )

    def unpack(ch):
        span = GROUP * MAIN
        tops = [
            blocks[ch, g * GROUP : (g + 1) * GROUP, :, 0:HALF].reshape(size, HALF)
            for g in range(groups)
        ]
        rests = [
            blocks[ch, g * GROUP : (g + 1) * GROUP, :, HALF:WIDE].reshape(size, PIECE)
            for g in range(groups)
        ]
        for g in range(groups):
            main = turned(tops[g], main_perm[...]).astype(jnp.bfloat16)
            for h in range(2):
                rows[h * HALF : (h + 1) * HALF, g * span : (g + 1) * span] = main[
                    :, h * span : (h + 1) * span
                ]
        for e in range(8):
            rest = sum(turned(rests[g], rest_perm[g * 8 + e]) for g in range(groups))
            rows[e * PIECE : (e + 1) * PIECE, n * MAIN : cols] = rest.astype(jnp.bfloat16)

    def tiles(extent, step, body, carry):
        full = extent // step
        carry = lax.fori_loop(
            0, full, lambda t, v: body(pl.multiple_of(t * step, step), step, v), carry
        )
        if extent % step:
            carry = body(full * step, extent % step, carry)
        return carry

    def partial(ch):
        head_copy(ch).wait()

        def body(begin, amount, peak):
            tile = dot(head[ch, pl.ds(begin, amount), :], rows[...])
            if ch > 0:
                tile = tile + scores[pl.ds(begin, amount), :]
            scores[pl.ds(begin, amount), :] = tile
            if ch == chunks - 1:
                peak = jnp.maximum(peak, jnp.max(tile, axis=0, keepdims=True))
            return peak

        return tiles(vocab, 512, body, jnp.full((1, cols), -jnp.inf, jnp.float32))

    padded = scores.shape[0]
    if padded > vocab:
        scores[vocab:padded, :] = jnp.full((padded - vocab, cols), -1e30, jnp.float32)

    across(0)
    if chunks > 2:
        column_on(2)
    if chunks > 1:
        across(1)
    for ch in range(chunks):
        if ch + 3 < chunks:
            column_on(ch + 3)
        if ch + 2 < chunks:
            across(ch + 2)
        settle(ch)
        unpack(ch)
        peak = partial(ch)

    @pl.loop(1, n)
    def _(p):
        other = (me + p) % n
        pltpu.make_async_remote_copy(
            src_ref=meta.at[other],
            dst_ref=meta.at[other],
            send_sem=meta_send.at[p],
            recv_sem=meta_recv.at[other],
            device_id={"tensor": other},
            device_id_type=MESH,
        ).wait_recv()

    ids = sum(meta[s, 0:1, :] for s in range(n))
    places = sum(meta[s, 1:2, :] for s in range(n)) - 1
    local_ids = ids - me * vocab
    local_ids = jnp.where(local_ids < vocab, local_ids, -1)

    def collect(begin, amount, carry):
        row_sum, spread, picked = carry
        tile = scores[pl.ds(begin, amount), :]
        centred = tile - peak
        expo = jnp.exp(centred)
        entry = begin + iota(tile.shape, 0)
        given = jnp.where(entry == local_ids, tile, 0.0)

        def fold(x):
            return jnp.sum(x.reshape(amount // 8, 8, cols), axis=0)

        return row_sum + fold(expo), spread + fold(expo * centred), picked + fold(given)

    nothing = jnp.zeros((8, cols), jnp.float32)
    row_sum, spread, picked = (
        jnp.sum(x, axis=0, keepdims=True)
        for x in tiles(padded, 64, collect, (nothing, nothing, nothing))
    )
    nothing = nothing[0:1]
    stats[me, 0:1, :] = peak
    stats[me, 1:2, :] = row_sum
    stats[me, 2:3, :] = spread
    stats[me, 3:4, :] = picked

    @pl.loop(1, n)
    def _(p):
        stat_copy(p).start()

    tall = iota((own_rows, cols), 0)
    mine = places == me * own_rows + tall
    kept = iota((seqs, 1), 0)
    first = jnp.zeros((seqs, 1), jnp.int32)
    length = jnp.ones((seqs, 1), jnp.int32)
    for k in range(seqs):
        first = jnp.where(kept == k, offsets_ref[k], first)
        length = jnp.where(kept == k, lengths_ref[k], length)
    inside = (places >= first) & (places < first + length)

    @pl.loop(1, n)
    def _(p):
        other = (me + p) % n
        pltpu.make_async_remote_copy(
            src_ref=stats.at[other],
            dst_ref=stats.at[other],
            send_sem=stat_send.at[p],
            recv_sem=stat_recv.at[other],
            device_id={"tensor": other},
            device_id_type=MESH,
        ).wait_recv()

    top = functools.reduce(jnp.maximum, [stats[s, 0:1, :] for s in range(n)])
    sum_exp, spread, picked = nothing, nothing, nothing
    for s in range(n):
        shift = stats[s, 0:1, :] - top
        factor = jnp.exp(shift)
        part = stats[s, 1:2, :]
        sum_exp = sum_exp + factor * part
        spread = spread + factor * (stats[s, 2:3, :] + shift * part)
        picked = picked + stats[s, 3:4, :]
    log_total = jnp.log(sum_exp)
    logprob = picked - top - log_total
    entropy = log_total - spread / sum_exp

    def lay(col):
        amount = col.shape[0]
        square = iota((amount, amount), 0) == iota((amount, amount), 1)
        return jnp.sum(jnp.where(square, col, 0.0), axis=0, keepdims=True)

    def total(where, value):
        return jnp.sum(jnp.where(where, value, 0.0), axis=1, keepdims=True)

    result_ref[0:1, 0:own_rows] = lay(total(mine, logprob))
    result_ref[1:2, 0:own_rows] = lay(total(mine, entropy))
    result_ref[2:3, 0:seqs] = lay(total(inside, logprob) / length.astype(jnp.float32))

    for ch in range(chunks):
        for slot in range(slots[ch]):
            remote(ch, me, slot, (me + 1) % n).wait_send()

    @pl.loop(1, n)
    def _(p):
        meta_copy(p).wait_send()
        stat_copy(p).wait_send()


def local(n, hidden, norm_gain, head_weight, targets, lengths, offsets, loss_mask):
    own_rows, width = hidden.shape
    vocab = head_weight.shape[0]
    seqs = lengths.shape[0]
    chunks = width // CHUNK
    cols = n * MAIN + 128
    hbm = pl.BlockSpec(memory_space=pltpu.HBM)
    vmem = pl.BlockSpec(memory_space=pltpu.VMEM)
    dma = pltpu.SemaphoreType.DMA
    result = pl.pallas_call(
        functools.partial(kernel, n),
        out_shape=jax.ShapeDtypeStruct((8, 128), jnp.float32),
        in_specs=[hbm] * 7,
        out_specs=vmem,
        scratch_shapes=[
            pltpu.SMEM((own_rows,), jnp.int32),
            pltpu.SMEM((seqs,), jnp.int32),
            pltpu.SMEM((seqs,), jnp.int32),
            pltpu.SMEM((own_rows,), jnp.int32),
            pltpu.VMEM((own_rows, width), jnp.bfloat16),
            pltpu.VMEM((width,), jnp.float32),
            pltpu.VMEM((chunks, vocab, CHUNK), jnp.bfloat16),
            pltpu.VMEM((chunks, n, TOK, WIDE), jnp.bfloat16),
            pltpu.VMEM((GROUP * TOK, GROUP * TOK), jnp.bfloat16),
            pltpu.VMEM((n // GROUP * 8, GROUP * TOK, 128), jnp.bfloat16),
            pltpu.VMEM((CHUNK, cols), jnp.bfloat16),
            pltpu.VMEM((-(-vocab // 8) * 8, cols), jnp.float32),
            pltpu.VMEM((n, 2, cols), jnp.int32),
            pltpu.VMEM((n, 4, cols), jnp.float32),
            dma((6,)),
            dma((chunks,)),
            dma((chunks, n)),
            dma((chunks, n)),
            dma((n,)),
            dma((n,)),
            dma((n,)),
            dma((n,)),
        ],
        compiler_params=pltpu.CompilerParams(
            collective_id=0, has_side_effects=True, vmem_limit_bytes=64 * 2**20
        ),
        cost_estimate=pl.CostEstimate(
            flops=2 * vocab * width * n * LIVE,
            bytes_accessed=2 * vocab * width,
            transcendentals=vocab * n * LIVE,
        ),
        name="head_stats",
    )(targets, lengths, offsets, loss_mask, hidden, norm_gain, head_weight)
    sizes = (own_rows, own_rows, seqs)

    def split(packed_ref, *out_refs):
        for i, size in enumerate(sizes):
            out_refs[i][...] = packed_ref[i, 0:size]

    return pl.pallas_call(
        split,
        out_shape=tuple(jax.ShapeDtypeStruct((size,), jnp.float32) for size in sizes),
        in_specs=[vmem],
        out_specs=(vmem, vmem, vmem),
        compiler_params=pltpu.CompilerParams(vmem_limit_bytes=64 * 2**20),
        name="split",
    )(result)


def solution(mesh):
    return jax.shard_map(
        functools.partial(local, mesh.shape["tensor"]),
        mesh=mesh,
        in_specs=(
            P(("dp", "tensor"), None),
            P(),
            P(("dp", "tensor"), None),
            P(("dp", "tensor")),
            P("dp"),
            P("dp"),
            P(("dp", "tensor")),
        ),
        out_specs=(P(("dp", "tensor")), P(("dp", "tensor")), P("dp")),
        check_vma=False,
    )
```

```python
import functools

import jax
import jax.numpy as jnp
from jax import lax
from jax.experimental import pallas as pl
from jax.experimental.pallas import tpu as pltpu
from jax.sharding import PartitionSpec as P

epsilon = 1e-05
LIVE = 10
MAIN = 8
REST = LIVE - MAIN
TOK = 16
CHUNK = 1024
HALF = CHUNK // 2
PIECE = CHUNK // 8
WIDE = HALF + PIECE
GROUP = 16
MESH = pl.DeviceIdType.MESH


def grid_dims(n):
    return {16: (4, 2, 2), 64: (4, 4, 4)}[n]


def iota(shape, dim):
    return lax.broadcasted_iota(jnp.int32, shape, dim)


def kernel(
    n,
    targets_hbm,
    lengths_hbm,
    offsets_hbm,
    mask_hbm,
    hidden_hbm,
    gain_hbm,
    weight_ref,
    result_ref,
    targets_ref,
    lengths_ref,
    offsets_ref,
    mask_ref,
    hidden_ref,
    gain_ref,
    head,
    blocks,
    main_perm,
    rest_perm,
    rows,
    scores,
    meta,
    stats,
    in_sem,
    head_sem,
    send_sem,
    recv_sem,
    meta_send,
    meta_recv,
    stat_send,
    stat_recv,
):
    vocab = weight_ref.shape[0]
    own_rows, width = hidden_ref.shape
    seqs = lengths_ref.shape[0]
    chunks = width // CHUNK
    cols = rows.shape[1]
    na, nb, nc = grid_dims(n)
    me = lax.axis_index("tensor")
    a = me // (nb * nc)
    b = (me // nc) % nb
    c = me % nc

    def at(i, j, k):
        return ((a + i) % na) * (nb * nc) + ((b + j) % nb) * nc + (c + k) % nc

    def slot_of(j, k):
        return (((b + j) % nb) * nc + (c + k) % nc) * na

    mine_at = slot_of(0, 0)

    def head_copy(ch):
        return pltpu.make_async_copy(
            weight_ref.at[:, pl.ds(ch * CHUNK, CHUNK)], head.at[ch], head_sem.at[ch]
        )

    barrier = pltpu.get_barrier_semaphore()

    @pl.loop(1, n)
    def _(p):
        pl.semaphore_signal(
            barrier, inc=1, device_id={"tensor": (me + p) % n}, device_id_type=MESH
        )

    small = [
        pltpu.make_async_copy(there, here, in_sem.at[i])
        for i, (there, here) in enumerate(
            (
                (hidden_hbm, hidden_ref),
                (gain_hbm, gain_ref),
                (mask_hbm, mask_ref),
                (targets_hbm, targets_ref),
                (lengths_hbm, lengths_ref),
                (offsets_hbm, offsets_ref),
            )
        )
    ]
    for copy in small:
        copy.start()
    for ch in range(chunks):
        head_copy(ch).start()
    for copy in small:
        copy.wait()

    values = hidden_ref[...].astype(jnp.float32)
    meansq = jnp.mean(values * values, axis=1, keepdims=True)
    normed = (values * lax.rsqrt(meansq + epsilon) * gain_ref[...][None, :]).astype(jnp.bfloat16)

    sub = iota((TOK, own_rows), 0)
    lane = iota((TOK, own_rows), 1)
    rank_of = jnp.full((TOK, own_rows), -1, jnp.int32)
    ranks = []
    count = jnp.int32(0)
    for i in range(own_rows):
        live = mask_ref[i]
        ranks.append(jnp.where(live == 1, count, -2))
        count = count + live
        rank_of = jnp.where(lane == i, ranks[i], rank_of)

    def choice(begin, first, amount):
        hit = (sub >= begin) & (sub < begin + amount) & (rank_of == sub - begin + first)
        return jnp.where(hit, 1.0, 0.0).astype(jnp.bfloat16)

    def dot(x, y):
        return jnp.dot(x, y, preferred_element_type=jnp.float32)

    halves = [choice(h * MAIN, 0, MAIN) for h in range(2)]
    pieces = [choice(e * REST, MAIN, REST) for e in range(8)]

    def pack(ch):
        base = ch * CHUNK
        packed = sum(
            dot(halves[h], normed[:, base + h * HALF : base + (h + 1) * HALF]) for h in range(2)
        )
        blocks[ch, mine_at, :, 0:HALF] = packed.astype(jnp.bfloat16)
        packed = sum(
            dot(pieces[e], normed[:, base + e * PIECE : base + (e + 1) * PIECE]) for e in range(8)
        )
        blocks[ch, mine_at, :, HALF:WIDE] = packed.astype(jnp.bfloat16)

    sent = [[] for ch in range(chunks)]

    def remote(ch, begin, end, amount, slot, peer):
        return pltpu.make_async_remote_copy(
            src_ref=blocks.at[ch, pl.ds(begin, amount)],
            dst_ref=blocks.at[ch, pl.ds(end, amount)],
            send_sem=send_sem.at[ch, slot],
            recv_sem=recv_sem.at[ch, end],
            device_id={"tensor": peer},
            device_id_type=MESH,
        )

    def send(ch, begin, end, amount, peer):
        remote(ch, begin, end, amount, len(sent[ch]), peer).start()
        sent[ch].append(amount)

    def arrive(ch, begin, amount):
        remote(ch, begin, begin, amount, 0, (me + 1) % n).wait_recv()

    def to_b(ch, begin, amount):
        for j in range(1, nb):
            send(ch, begin, begin, amount, at(0, j, 0))

    def to_c(ch, begin, amount):
        for k in range(1, nc):
            send(ch, begin, begin, amount, at(0, 0, k))

    def along_a(ch):
        for i in range(1, na):
            send(ch, mine_at, mine_at + na - i, 1, at(i, 0, 0))

    def own(ch):
        to_b(ch, mine_at, 1)
        to_c(ch, mine_at, 1)

    def column_on(ch):
        for i in range(1, na):
            arrive(ch, mine_at + i, 1)
        to_b(ch, mine_at + 1, na - 1)
        to_c(ch, mine_at + 1, na - 1)

    early = na // 2

    def across(ch):
        for j in range(1, nb):
            arrive(ch, slot_of(j, 0), 1)
            arrive(ch, slot_of(j, 0) + 1, na - 1)
            to_c(ch, slot_of(j, 0), early)
        for k in range(1, nc):
            arrive(ch, slot_of(0, k), 1)
            arrive(ch, slot_of(0, k) + 1, na - 1)
            to_b(ch, slot_of(0, k) + early, na - early)

    def settle(ch):
        for j in range(1, nb):
            for k in range(1, nc):
                arrive(ch, slot_of(j, k), early)
                arrive(ch, slot_of(j, k) + early, na - early)

    def meta_copy(p):
        return pltpu.make_async_remote_copy(
            src_ref=meta.at[me],
            dst_ref=meta.at[me],
            send_sem=meta_send.at[p],
            recv_sem=meta_recv.at[me],
            device_id={"tensor": (me + p) % n},
            device_id_type=MESH,
        )

    def stat_copy(p):
        return pltpu.make_async_remote_copy(
            src_ref=stats.at[me],
            dst_ref=stats.at[me],
            send_sem=stat_send.at[p],
            recv_sem=stat_recv.at[me],
            device_id={"tensor": (me + p) % n},
            device_id_type=MESH,
        )

    pack(0)
    pl.semaphore_wait(barrier, n - 1)
    along_a(0)
    own(0)
    for ch in range(1, chunks):
        pack(ch)
        along_a(ch)
        own(ch)

    column = iota((1, cols), 1)
    in_main = column < n * MAIN
    owner = jnp.where(in_main, column // MAIN, (column - n * MAIN) // REST)
    rank_at = jnp.where(in_main, column % MAIN, MAIN + (column - n * MAIN) % REST)
    rank_at = jnp.where(owner == mine_at + a, rank_at, -1)
    ids = jnp.zeros((1, cols), jnp.int32)
    places = jnp.zeros((1, cols), jnp.int32)
    for i in range(own_rows):
        ids = jnp.where(rank_at == ranks[i], targets_ref[i], ids)
        places = jnp.where(rank_at == ranks[i], me * own_rows + (i + 1), places)
    meta[me, 0:1, :] = ids
    meta[me, 1:2, :] = places

    @pl.loop(1, n)
    def _(p):
        meta_copy(p).start()

    column_on(0)
    if chunks > 1:
        column_on(1)

    def slot_at(block):
        return block // na * na + (block % na + na - a) % na

    groups = n // GROUP
    size = GROUP * TOK
    in_row = iota((size, size), 0)
    out_col = iota((size, size), 1)
    span = GROUP * MAIN
    source = slot_at((out_col % span) // MAIN) * TOK + out_col // span * MAIN + out_col % MAIN
    main_perm[...] = jnp.where(in_row == source, 1.0, 0.0).astype(jnp.bfloat16)
    tail = cols - n * MAIN
    in_row = iota((size, tail), 0)
    for g in range(groups):
        out_col = iota((size, tail), 1) - g * GROUP * REST
        valid = (out_col >= 0) & (out_col < GROUP * REST)
        out_col = jnp.maximum(out_col, 0)
        for e in range(8):
            source = slot_at(out_col // REST) * TOK + e * REST + out_col % REST
            rest_perm[g * 8 + e] = jnp.where(valid & (in_row == source), 1.0, 0.0).astype(
                jnp.bfloat16
            )

    def turned(x, y):
        return lax.dot_general(
            x, y, (((0,), (0,)), ((), ())), preferred_element_type=jnp.float32
        )

    def unpack(ch):
        span = GROUP * MAIN
        tops = [
            blocks[ch, g * GROUP : (g + 1) * GROUP, :, 0:HALF].reshape(size, HALF)
            for g in range(groups)
        ]
        rests = [
            blocks[ch, g * GROUP : (g + 1) * GROUP, :, HALF:WIDE].reshape(size, PIECE)
            for g in range(groups)
        ]
        for g in range(groups):
            main = turned(tops[g], main_perm[...]).astype(jnp.bfloat16)
            for h in range(2):
                rows[h * HALF : (h + 1) * HALF, g * span : (g + 1) * span] = main[
                    :, h * span : (h + 1) * span
                ]
        for e in range(8):
            rest = sum(turned(rests[g], rest_perm[g * 8 + e]) for g in range(groups))
            rows[e * PIECE : (e + 1) * PIECE, n * MAIN : cols] = rest.astype(jnp.bfloat16)

    def tiles(extent, step, body, carry):
        full = extent // step
        carry = lax.fori_loop(
            0, full, lambda t, v: body(pl.multiple_of(t * step, step), step, v), carry
        )
        if extent % step:
            carry = body(full * step, extent % step, carry)
        return carry

    def partial(ch):
        head_copy(ch).wait()

        def body(begin, amount, peak):
            tile = dot(head[ch, pl.ds(begin, amount), :], rows[...])
            if ch > 0:
                tile = tile + scores[pl.ds(begin, amount), :]
            scores[pl.ds(begin, amount), :] = tile
            if ch == chunks - 1:
                peak = jnp.maximum(peak, jnp.max(tile, axis=0, keepdims=True))
            return peak

        peak = jnp.full((1, cols), -jnp.inf, jnp.float32)
        for begin in range(0, vocab, 512):
            peak = body(begin, min(512, vocab - begin), peak)
        return peak

    padded = scores.shape[0]
    if padded > vocab:
        scores[vocab:padded, :] = jnp.full((padded - vocab, cols), -1e30, jnp.float32)

    across(0)
    if chunks > 2:
        column_on(2)
    if chunks > 1:
        across(1)
    for ch in range(chunks):
        if ch + 3 < chunks:
            column_on(ch + 3)
        if ch + 2 < chunks:
            across(ch + 2)
        settle(ch)
        unpack(ch)
        peak = partial(ch)

    @pl.loop(1, n)
    def _(p):
        other = (me + p) % n
        pltpu.make_async_remote_copy(
            src_ref=meta.at[other],
            dst_ref=meta.at[other],
            send_sem=meta_send.at[p],
            recv_sem=meta_recv.at[other],
            device_id={"tensor": other},
            device_id_type=MESH,
        ).wait_recv()

    ids = sum(meta[s, 0:1, :] for s in range(n))
    places = sum(meta[s, 1:2, :] for s in range(n)) - 1
    local_ids = ids - me * vocab
    local_ids = jnp.where(local_ids < vocab, local_ids, -1)

    def collect(begin, amount, carry):
        row_sum, spread, picked = carry
        tile = scores[pl.ds(begin, amount), :]
        centred = tile - peak
        expo = jnp.exp(centred)
        entry = begin + iota(tile.shape, 0)
        given = jnp.where(entry == local_ids, tile, 0.0)

        def fold(x):
            return jnp.sum(x.reshape(amount // 8, 8, cols), axis=0)

        return row_sum + fold(expo), spread + fold(expo * centred), picked + fold(given)

    nothing = jnp.zeros((8, cols), jnp.float32)
    row_sum, spread, picked = (
        jnp.sum(x, axis=0, keepdims=True)
        for x in tiles(padded, 64, collect, (nothing, nothing, nothing))
    )
    nothing = nothing[0:1]
    stats[me, 0:1, :] = peak
    stats[me, 1:2, :] = row_sum
    stats[me, 2:3, :] = spread
    stats[me, 3:4, :] = picked

    @pl.loop(1, n)
    def _(p):
        stat_copy(p).start()

    tall = iota((own_rows, cols), 0)
    mine = places == me * own_rows + tall
    kept = iota((seqs, 1), 0)
    first = jnp.zeros((seqs, 1), jnp.int32)
    length = jnp.ones((seqs, 1), jnp.int32)
    for k in range(seqs):
        first = jnp.where(kept == k, offsets_ref[k], first)
        length = jnp.where(kept == k, lengths_ref[k], length)
    inside = (places >= first) & (places < first + length)

    @pl.loop(1, n)
    def _(p):
        other = (me + p) % n
        pltpu.make_async_remote_copy(
            src_ref=stats.at[other],
            dst_ref=stats.at[other],
            send_sem=stat_send.at[p],
            recv_sem=stat_recv.at[other],
            device_id={"tensor": other},
            device_id_type=MESH,
        ).wait_recv()

    top = functools.reduce(jnp.maximum, [stats[s, 0:1, :] for s in range(n)])
    sum_exp, spread, picked = nothing, nothing, nothing
    for s in range(n):
        shift = stats[s, 0:1, :] - top
        factor = jnp.exp(shift)
        part = stats[s, 1:2, :]
        sum_exp = sum_exp + factor * part
        spread = spread + factor * (stats[s, 2:3, :] + shift * part)
        picked = picked + stats[s, 3:4, :]
    log_total = jnp.log(sum_exp)
    logprob = picked - top - log_total
    entropy = log_total - spread / sum_exp

    def lay(col):
        amount = col.shape[0]
        square = iota((amount, amount), 0) == iota((amount, amount), 1)
        return jnp.sum(jnp.where(square, col, 0.0), axis=0, keepdims=True)

    def total(where, value):
        return jnp.sum(jnp.where(where, value, 0.0), axis=1, keepdims=True)

    result_ref[0:1, 0:own_rows] = lay(total(mine, logprob))
    result_ref[1:2, 0:own_rows] = lay(total(mine, entropy))
    result_ref[2:3, 0:seqs] = lay(total(inside, logprob) / length.astype(jnp.float32))

    for ch in range(chunks):
        for slot, amount in enumerate(sent[ch]):
            remote(ch, 0, 0, amount, slot, (me + 1) % n).wait_send()

    @pl.loop(1, n)
    def _(p):
        meta_copy(p).wait_send()
        stat_copy(p).wait_send()


def local(n, hidden, norm_gain, head_weight, targets, lengths, offsets, loss_mask):
    own_rows, width = hidden.shape
    vocab = head_weight.shape[0]
    seqs = lengths.shape[0]
    chunks = width // CHUNK
    cols = n * MAIN + 128
    hbm = pl.BlockSpec(memory_space=pltpu.HBM)
    vmem = pl.BlockSpec(memory_space=pltpu.VMEM)
    dma = pltpu.SemaphoreType.DMA
    result = pl.pallas_call(
        functools.partial(kernel, n),
        out_shape=jax.ShapeDtypeStruct((8, 128), jnp.float32),
        in_specs=[hbm] * 7,
        out_specs=vmem,
        scratch_shapes=[
            pltpu.SMEM((own_rows,), jnp.int32),
            pltpu.SMEM((seqs,), jnp.int32),
            pltpu.SMEM((seqs,), jnp.int32),
            pltpu.SMEM((own_rows,), jnp.int32),
            pltpu.VMEM((own_rows, width), jnp.bfloat16),
            pltpu.VMEM((width,), jnp.float32),
            pltpu.VMEM((chunks, vocab, CHUNK), jnp.bfloat16),
            pltpu.VMEM((chunks, n, TOK, WIDE), jnp.bfloat16),
            pltpu.VMEM((GROUP * TOK, GROUP * TOK), jnp.bfloat16),
            pltpu.VMEM((n // GROUP * 8, GROUP * TOK, 128), jnp.bfloat16),
            pltpu.VMEM((CHUNK, cols), jnp.bfloat16),
            pltpu.VMEM((-(-vocab // 8) * 8, cols), jnp.float32),
            pltpu.VMEM((n, 2, cols), jnp.int32),
            pltpu.VMEM((n, 4, cols), jnp.float32),
            dma((6,)),
            dma((chunks,)),
            dma((chunks, n)),
            dma((chunks, n)),
            dma((n,)),
            dma((n,)),
            dma((n,)),
            dma((n,)),
        ],
        compiler_params=pltpu.CompilerParams(
            collective_id=0, has_side_effects=True, vmem_limit_bytes=64 * 2**20
        ),
        cost_estimate=pl.CostEstimate(
            flops=2 * vocab * width * n * LIVE,
            bytes_accessed=2 * vocab * width,
            transcendentals=vocab * n * LIVE,
        ),
        name="head_stats",
    )(targets, lengths, offsets, loss_mask, hidden, norm_gain, head_weight)
    sizes = (own_rows, own_rows, seqs)

    def split(packed_ref, *out_refs):
        for i, size in enumerate(sizes):
            out_refs[i][...] = packed_ref[i, 0:size]

    return pl.pallas_call(
        split,
        out_shape=tuple(jax.ShapeDtypeStruct((size,), jnp.float32) for size in sizes),
        in_specs=[vmem],
        out_specs=(vmem, vmem, vmem),
        compiler_params=pltpu.CompilerParams(vmem_limit_bytes=64 * 2**20),
        name="split",
    )(result)


def solution(mesh):
    return jax.shard_map(
        functools.partial(local, mesh.shape["tensor"]),
        mesh=mesh,
        in_specs=(
            P(("dp", "tensor"), None),
            P(),
            P(("dp", "tensor"), None),
            P(("dp", "tensor")),
            P("dp"),
            P("dp"),
            P(("dp", "tensor")),
        ),
        out_specs=(P(("dp", "tensor")), P(("dp", "tensor")), P("dp")),
        check_vma=False,
    )
```

```python
import functools

import jax
import jax.numpy as jnp
from jax import lax
from jax.experimental import pallas as pl
from jax.experimental.pallas import tpu as pltpu
from jax.sharding import PartitionSpec as P

epsilon = 1e-05
LIVE = 10
MAIN = 8
REST = LIVE - MAIN
TOK = 16
CHUNK = 1024
HALF = CHUNK // 2
PIECE = CHUNK // 8
WIDE = HALF + PIECE
GROUP = 16
MESH = pl.DeviceIdType.MESH


def grid_dims(n):
    return {16: (4, 2, 2), 64: (4, 4, 4)}[n]


def iota(shape, dim):
    return lax.broadcasted_iota(jnp.int32, shape, dim)


def kernel(
    n,
    targets_hbm,
    lengths_hbm,
    offsets_hbm,
    mask_hbm,
    hidden_hbm,
    gain_hbm,
    weight_ref,
    result_ref,
    targets_ref,
    lengths_ref,
    offsets_ref,
    mask_ref,
    hidden_ref,
    gain_ref,
    head,
    blocks,
    main_perm,
    rest_perm,
    rows,
    scores,
    meta,
    stats,
    in_sem,
    head_sem,
    send_sem,
    recv_sem,
    meta_send,
    meta_recv,
    stat_send,
    stat_recv,
):
    vocab = weight_ref.shape[0]
    own_rows, width = hidden_ref.shape
    seqs = lengths_ref.shape[0]
    chunks = width // CHUNK
    cols = rows.shape[1]
    na, nb, nc = grid_dims(n)
    me = lax.axis_index("tensor")
    a = me // (nb * nc)
    b = (me // nc) % nb
    c = me % nc

    def at(i, j, k):
        return ((a + i) % na) * (nb * nc) + ((b + j) % nb) * nc + (c + k) % nc

    def slot_of(j, k):
        return (((b + j) % nb) * nc + (c + k) % nc) * na

    mine_at = slot_of(0, 0)

    def head_copy(ch):
        return pltpu.make_async_copy(
            weight_ref.at[:, pl.ds(ch * CHUNK, CHUNK)], head.at[ch], head_sem.at[ch]
        )

    barrier = pltpu.get_barrier_semaphore()

    @pl.loop(1, n)
    def _(p):
        pl.semaphore_signal(
            barrier, inc=1, device_id={"tensor": (me + p) % n}, device_id_type=MESH
        )

    small = [
        pltpu.make_async_copy(there, here, in_sem.at[i])
        for i, (there, here) in enumerate(
            (
                (hidden_hbm, hidden_ref),
                (gain_hbm, gain_ref),
                (mask_hbm, mask_ref),
                (targets_hbm, targets_ref),
                (lengths_hbm, lengths_ref),
                (offsets_hbm, offsets_ref),
            )
        )
    ]
    for copy in small:
        copy.start()
    for ch in range(chunks):
        head_copy(ch).start()
    for copy in small:
        copy.wait()

    values = hidden_ref[...].astype(jnp.float32)
    meansq = jnp.mean(values * values, axis=1, keepdims=True)
    normed = (values * lax.rsqrt(meansq + epsilon) * gain_ref[...][None, :]).astype(jnp.bfloat16)

    sub = iota((TOK, 8 * own_rows), 0)
    lane = iota((TOK, 8 * own_rows), 1)
    rank_of = jnp.full((TOK, 8 * own_rows), -1, jnp.int32)
    ranks = []
    count = jnp.int32(0)
    for i in range(own_rows):
        live = mask_ref[i]
        ranks.append(jnp.where(live == 1, count, -2))
        count = count + live
        rank_of = jnp.where(lane % own_rows == i, ranks[i], rank_of)

    def choice(first, amount):
        hit = (sub // amount == lane // own_rows) & (rank_of == first + sub % amount)
        return jnp.where(hit, 1.0, 0.0).astype(jnp.bfloat16)

    def dot(x, y):
        return jnp.dot(x, y, preferred_element_type=jnp.float32)

    halves = choice(0, MAIN)[:, 0 : 2 * own_rows]
    pieces = choice(MAIN, REST)

    def stack(begin, step, amount):
        parts = [normed[:, begin + e * step : begin + (e + 1) * step] for e in range(amount)]
        return jnp.concatenate(parts, axis=0)

    def pack(ch):
        packed = dot(halves, stack(ch * CHUNK, HALF, 2))
        blocks[ch, mine_at, :, 0:HALF] = packed.astype(jnp.bfloat16)
        packed = dot(pieces, stack(ch * CHUNK, PIECE, 8))
        blocks[ch, mine_at, :, HALF:WIDE] = packed.astype(jnp.bfloat16)

    sent = [[] for ch in range(chunks)]

    def remote(ch, begin, end, amount, slot, peer):
        return pltpu.make_async_remote_copy(
            src_ref=blocks.at[ch, pl.ds(begin, amount)],
            dst_ref=blocks.at[ch, pl.ds(end, amount)],
            send_sem=send_sem.at[ch, slot],
            recv_sem=recv_sem.at[ch, end],
            device_id={"tensor": peer},
            device_id_type=MESH,
        )

    def send(ch, begin, end, amount, peer):
        remote(ch, begin, end, amount, len(sent[ch]), peer).start()
        sent[ch].append(amount)

    def arrive(ch, begin, amount):
        remote(ch, begin, begin, amount, 0, (me + 1) % n).wait_recv()

    def to_b(ch, begin, amount):
        for j in range(1, nb):
            send(ch, begin, begin, amount, at(0, j, 0))

    def to_c(ch, begin, amount):
        for k in range(1, nc):
            send(ch, begin, begin, amount, at(0, 0, k))

    def along_a(ch):
        for i in range(1, na):
            send(ch, mine_at, mine_at + na - i, 1, at(i, 0, 0))

    def own(ch):
        to_b(ch, mine_at, 1)
        to_c(ch, mine_at, 1)

    def column_on(ch):
        for i in range(1, na):
            arrive(ch, mine_at + i, 1)
        to_b(ch, mine_at + 1, na - 1)
        to_c(ch, mine_at + 1, na - 1)

    early = na // 2

    def across(ch):
        for j in range(1, nb):
            arrive(ch, slot_of(j, 0), 1)
            arrive(ch, slot_of(j, 0) + 1, na - 1)
            to_c(ch, slot_of(j, 0), early)
        for k in range(1, nc):
            arrive(ch, slot_of(0, k), 1)
            arrive(ch, slot_of(0, k) + 1, na - 1)
            to_b(ch, slot_of(0, k) + early, na - early)

    def settle(ch):
        for j in range(1, nb):
            for k in range(1, nc):
                arrive(ch, slot_of(j, k), early)
                arrive(ch, slot_of(j, k) + early, na - early)

    def meta_copy(p):
        return pltpu.make_async_remote_copy(
            src_ref=meta.at[me],
            dst_ref=meta.at[me],
            send_sem=meta_send.at[p],
            recv_sem=meta_recv.at[me],
            device_id={"tensor": (me + p) % n},
            device_id_type=MESH,
        )

    def stat_copy(p):
        return pltpu.make_async_remote_copy(
            src_ref=stats.at[me],
            dst_ref=stats.at[me],
            send_sem=stat_send.at[p],
            recv_sem=stat_recv.at[me],
            device_id={"tensor": (me + p) % n},
            device_id_type=MESH,
        )

    pack(0)
    pl.semaphore_wait(barrier, n - 1)
    along_a(0)
    own(0)
    for ch in range(1, chunks):
        pack(ch)
        along_a(ch)
        own(ch)
        if ch == 2:
            column_on(0)
    column_on(1)

    across(0)

    def slot_at(block):
        return block // na * na + (block % na + na - a) % na

    groups = n // GROUP
    size = GROUP * TOK
    in_row = iota((size, size), 0)
    out_col = iota((size, size), 1)
    span = GROUP * MAIN
    source = slot_at((out_col % span) // MAIN) * TOK + out_col // span * MAIN + out_col % MAIN
    main_perm[...] = jnp.where(in_row == source, 1.0, 0.0).astype(jnp.bfloat16)
    tail = cols - n * MAIN
    in_row = iota((size, tail), 0)
    for g in range(groups):
        out_col = iota((size, tail), 1) - g * GROUP * REST
        valid = (out_col >= 0) & (out_col < GROUP * REST)
        out_col = jnp.maximum(out_col, 0)
        for e in range(8):
            source = slot_at(out_col // REST) * TOK + e * REST + out_col % REST
            rest_perm[g * 8 + e] = jnp.where(valid & (in_row == source), 1.0, 0.0).astype(
                jnp.bfloat16
            )

    def turned(x, y):
        return lax.dot_general(
            x, y, (((0,), (0,)), ((), ())), preferred_element_type=jnp.float32
        )

    def unpack(ch):
        span = GROUP * MAIN
        tops = [
            blocks[ch, g * GROUP : (g + 1) * GROUP, :, 0:HALF].reshape(size, HALF)
            for g in range(groups)
        ]
        rests = [
            blocks[ch, g * GROUP : (g + 1) * GROUP, :, HALF:WIDE].reshape(size, PIECE)
            for g in range(groups)
        ]
        for g in range(groups):
            main = turned(tops[g], main_perm[...]).astype(jnp.bfloat16)
            for h in range(2):
                rows[h * HALF : (h + 1) * HALF, g * span : (g + 1) * span] = main[
                    :, h * span : (h + 1) * span
                ]
        for e in range(8):
            rest = sum(turned(rests[g], rest_perm[g * 8 + e]) for g in range(groups))
            rows[e * PIECE : (e + 1) * PIECE, n * MAIN : cols] = rest.astype(jnp.bfloat16)

    padded = scores.shape[0]

    def partial(ch):
        head_copy(ch).wait()
        found = []
        for begin in range(0, vocab, 512):
            amount = min(512, vocab - begin)
            tile = dot(head[ch, begin : begin + amount, :], rows[...])
            if ch > 0:
                tile = tile + scores[begin : begin + amount, :]
            scores[begin : begin + amount, :] = tile
            if ch == chunks - 1:
                peak = jnp.max(tile, axis=0, keepdims=True)
                found.append((peak,) + collect(begin, min(begin + 512, padded), peak))
        return found

    def collect(begin, end, peak):
        gathered = [jnp.zeros((8, cols), jnp.float32)] * 3
        for at_row in range(begin, end, 64):
            tile = scores[at_row : min(at_row + 64, end), :]
            centred = tile - peak
            expo = jnp.exp(centred)
            entry = at_row + iota(tile.shape, 0)
            given = jnp.where(entry == local_ids, tile, 0.0)
            gathered = [
                old + jnp.sum(x.reshape(x.shape[0] // 8, 8, cols), axis=0)
                for old, x in zip(gathered, (expo, expo * centred, given))
            ]
        return tuple(jnp.sum(x, axis=0, keepdims=True) for x in gathered)

    def merge(parts):
        peak = functools.reduce(jnp.maximum, [part[0] for part in parts])
        row_sum = spread = picked = 0.0
        for part in parts:
            shift = part[0] - peak
            factor = jnp.exp(shift)
            row_sum = row_sum + factor * part[1]
            spread = spread + factor * (part[2] + shift * part[1])
            picked = picked + part[3]
        return peak, row_sum, spread, picked

    if padded > vocab:
        scores[vocab:padded, :] = jnp.full((padded - vocab, cols), -1e30, jnp.float32)

    column = iota((1, cols), 1)
    in_main = column < n * MAIN
    owner = jnp.where(in_main, column // MAIN, (column - n * MAIN) // REST)
    rank_at = jnp.where(in_main, column % MAIN, MAIN + (column - n * MAIN) % REST)
    rank_at = jnp.where(owner == mine_at + a, rank_at, -1)
    ids = jnp.zeros((1, cols), jnp.int32)
    places = jnp.zeros((1, cols), jnp.int32)
    for i in range(own_rows):
        ids = jnp.where(rank_at == ranks[i], targets_ref[i], ids)
        places = jnp.where(rank_at == ranks[i], me * own_rows + (i + 1), places)
    meta[me, 0:1, :] = ids
    meta[me, 1:2, :] = places

    @pl.loop(1, n)
    def _(p):
        meta_copy(p).start()

    column_on(2)
    across(1)
    for ch in range(chunks):
        if ch + 3 < chunks:
            column_on(ch + 3)
        if ch + 2 < chunks:
            across(ch + 2)
        if ch + 1 < chunks:
            settle(ch)
            unpack(ch)
            partial(ch)

    @pl.loop(1, n)
    def _(p):
        other = (me + p) % n
        pltpu.make_async_remote_copy(
            src_ref=meta.at[other],
            dst_ref=meta.at[other],
            send_sem=meta_send.at[p],
            recv_sem=meta_recv.at[other],
            device_id={"tensor": other},
            device_id_type=MESH,
        ).wait_recv()

    ids = sum(meta[s, 0:1, :] for s in range(n))
    places = sum(meta[s, 1:2, :] for s in range(n)) - 1
    local_ids = ids - me * vocab
    local_ids = jnp.where(local_ids < vocab, local_ids, -1)
    settle(chunks - 1)
    unpack(chunks - 1)
    found = partial(chunks - 1)

    peak, row_sum, spread, picked = merge(found)
    stats[me, 0:1, :] = peak
    stats[me, 1:2, :] = row_sum
    stats[me, 2:3, :] = spread
    stats[me, 3:4, :] = picked

    @pl.loop(1, n)
    def _(p):
        stat_copy(p).start()

    tall = iota((own_rows, cols), 0)
    mine = places == me * own_rows + tall
    kept = iota((seqs, 1), 0)
    first = jnp.zeros((seqs, 1), jnp.int32)
    length = jnp.ones((seqs, 1), jnp.int32)
    for k in range(seqs):
        first = jnp.where(kept == k, offsets_ref[k], first)
        length = jnp.where(kept == k, lengths_ref[k], length)
    inside = (places >= first) & (places < first + length)

    @pl.loop(1, n)
    def _(p):
        other = (me + p) % n
        pltpu.make_async_remote_copy(
            src_ref=stats.at[other],
            dst_ref=stats.at[other],
            send_sem=stat_send.at[p],
            recv_sem=stat_recv.at[other],
            device_id={"tensor": other},
            device_id_type=MESH,
        ).wait_recv()

    top, sum_exp, spread, picked = merge(
        [tuple(stats[s, i : i + 1, :] for i in range(4)) for s in range(n)]
    )
    log_total = jnp.log(sum_exp)
    logprob = picked - top - log_total
    entropy = log_total - spread / sum_exp

    def lay(col):
        amount = col.shape[0]
        square = iota((amount, amount), 0) == iota((amount, amount), 1)
        return jnp.sum(jnp.where(square, col, 0.0), axis=0, keepdims=True)

    def total(where, value):
        return jnp.sum(jnp.where(where, value, 0.0), axis=1, keepdims=True)

    result_ref[0:1, 0:own_rows] = lay(total(mine, logprob))
    result_ref[1:2, 0:own_rows] = lay(total(mine, entropy))
    result_ref[2:3, 0:seqs] = lay(total(inside, logprob) / length.astype(jnp.float32))

    for ch in range(chunks):
        for slot, amount in enumerate(sent[ch]):
            remote(ch, 0, 0, amount, slot, (me + 1) % n).wait_send()

    @pl.loop(1, n)
    def _(p):
        meta_copy(p).wait_send()
        stat_copy(p).wait_send()


def local(n, hidden, norm_gain, head_weight, targets, lengths, offsets, loss_mask):
    own_rows, width = hidden.shape
    vocab = head_weight.shape[0]
    seqs = lengths.shape[0]
    chunks = width // CHUNK
    cols = n * MAIN + 128
    hbm = pl.BlockSpec(memory_space=pltpu.HBM)
    vmem = pl.BlockSpec(memory_space=pltpu.VMEM)
    dma = pltpu.SemaphoreType.DMA
    result = pl.pallas_call(
        functools.partial(kernel, n),
        out_shape=jax.ShapeDtypeStruct((8, 128), jnp.float32),
        in_specs=[hbm] * 7,
        out_specs=vmem,
        scratch_shapes=[
            pltpu.SMEM((own_rows,), jnp.int32),
            pltpu.SMEM((seqs,), jnp.int32),
            pltpu.SMEM((seqs,), jnp.int32),
            pltpu.SMEM((own_rows,), jnp.int32),
            pltpu.VMEM((own_rows, width), jnp.bfloat16),
            pltpu.VMEM((width,), jnp.float32),
            pltpu.VMEM((chunks, vocab, CHUNK), jnp.bfloat16),
            pltpu.VMEM((chunks, n, TOK, WIDE), jnp.bfloat16),
            pltpu.VMEM((GROUP * TOK, GROUP * TOK), jnp.bfloat16),
            pltpu.VMEM((n // GROUP * 8, GROUP * TOK, 128), jnp.bfloat16),
            pltpu.VMEM((CHUNK, cols), jnp.bfloat16),
            pltpu.VMEM((-(-vocab // 8) * 8, cols), jnp.float32),
            pltpu.VMEM((n, 2, cols), jnp.int32),
            pltpu.VMEM((n, 4, cols), jnp.float32),
            dma((6,)),
            dma((chunks,)),
            dma((chunks, n)),
            dma((chunks, n)),
            dma((n,)),
            dma((n,)),
            dma((n,)),
            dma((n,)),
        ],
        compiler_params=pltpu.CompilerParams(
            collective_id=0, has_side_effects=True, vmem_limit_bytes=64 * 2**20
        ),
        cost_estimate=pl.CostEstimate(
            flops=2 * vocab * width * n * LIVE,
            bytes_accessed=2 * vocab * width,
            transcendentals=vocab * n * LIVE,
        ),
        name="head_stats",
    )(targets, lengths, offsets, loss_mask, hidden, norm_gain, head_weight)
    sizes = (own_rows, own_rows, seqs)

    def split(packed_ref, *out_refs):
        for i, size in enumerate(sizes):
            out_refs[i][...] = packed_ref[i, 0:size]

    return pl.pallas_call(
        split,
        out_shape=tuple(jax.ShapeDtypeStruct((size,), jnp.float32) for size in sizes),
        in_specs=[vmem],
        out_specs=(vmem, vmem, vmem),
        compiler_params=pltpu.CompilerParams(vmem_limit_bytes=64 * 2**20),
        name="split",
    )(result)


def solution(mesh):
    return jax.shard_map(
        functools.partial(local, mesh.shape["tensor"]),
        mesh=mesh,
        in_specs=(
            P(("dp", "tensor"), None),
            P(),
            P(("dp", "tensor"), None),
            P(("dp", "tensor")),
            P("dp"),
            P("dp"),
            P(("dp", "tensor")),
        ),
        out_specs=(P(("dp", "tensor")), P(("dp", "tensor")), P("dp")),
        check_vma=False,
    )
```

```python
import functools

import jax
import jax.numpy as jnp
from jax import lax
from jax.experimental import pallas as pl
from jax.experimental.pallas import tpu as pltpu
from jax.sharding import PartitionSpec as P

epsilon = 1e-05
LIVE = 10
MAIN = 8
REST = LIVE - MAIN
TOK = 16
CHUNK = 2048
HALF = CHUNK // 2
PIECE = CHUNK // 8
WIDE = HALF + PIECE
GROUP = 16
MESH = pl.DeviceIdType.MESH


def grid_dims(n):
    return {16: (4, 2, 2), 64: (4, 4, 4)}[n]


def iota(shape, dim):
    return lax.broadcasted_iota(jnp.int32, shape, dim)


def kernel(
    n,
    targets_hbm,
    lengths_hbm,
    offsets_hbm,
    mask_hbm,
    hidden_hbm,
    gain_hbm,
    weight_ref,
    result_ref,
    targets_ref,
    lengths_ref,
    offsets_ref,
    mask_ref,
    hidden_ref,
    gain_ref,
    head,
    blocks,
    main_perm,
    rest_perm,
    rows,
    scores,
    meta,
    stats,
    in_sem,
    head_sem,
    send_sem,
    recv_sem,
    meta_send,
    meta_recv,
    stat_send,
    stat_recv,
):
    vocab = weight_ref.shape[0]
    own_rows, width = hidden_ref.shape
    seqs = lengths_ref.shape[0]
    chunks = width // CHUNK
    cols = rows.shape[1]
    na, nb, nc = grid_dims(n)
    me = lax.axis_index("tensor")
    a = me // (nb * nc)
    b = (me // nc) % nb
    c = me % nc

    def at(i, j, k):
        return ((a + i) % na) * (nb * nc) + ((b + j) % nb) * nc + (c + k) % nc

    def slot_of(j, k):
        return (((b + j) % nb) * nc + (c + k) % nc) * na

    mine_at = slot_of(0, 0)

    def head_copy(ch):
        return pltpu.make_async_copy(
            weight_ref.at[:, pl.ds(ch * CHUNK, CHUNK)], head.at[ch], head_sem.at[ch]
        )

    barrier = pltpu.get_barrier_semaphore()

    @pl.loop(1, n)
    def _(p):
        pl.semaphore_signal(
            barrier, inc=1, device_id={"tensor": (me + p) % n}, device_id_type=MESH
        )

    small = [
        pltpu.make_async_copy(there, here, in_sem.at[i])
        for i, (there, here) in enumerate(
            (
                (hidden_hbm, hidden_ref),
                (gain_hbm, gain_ref),
                (mask_hbm, mask_ref),
                (targets_hbm, targets_ref),
                (lengths_hbm, lengths_ref),
                (offsets_hbm, offsets_ref),
            )
        )
    ]
    for copy in small:
        copy.start()
    for ch in range(chunks):
        head_copy(ch).start()
    for copy in small:
        copy.wait()

    values = hidden_ref[...].astype(jnp.float32)
    meansq = jnp.mean(values * values, axis=1, keepdims=True)
    normed = (values * lax.rsqrt(meansq + epsilon) * gain_ref[...][None, :]).astype(jnp.bfloat16)

    sub = iota((TOK, 8 * own_rows), 0)
    lane = iota((TOK, 8 * own_rows), 1)
    rank_of = jnp.full((TOK, 8 * own_rows), -1, jnp.int32)
    ranks = []
    count = jnp.int32(0)
    for i in range(own_rows):
        live = mask_ref[i]
        ranks.append(jnp.where(live == 1, count, -2))
        count = count + live
        rank_of = jnp.where(lane % own_rows == i, ranks[i], rank_of)

    def choice(first, amount):
        hit = (sub // amount == lane // own_rows) & (rank_of == first + sub % amount)
        return jnp.where(hit, 1.0, 0.0).astype(jnp.bfloat16)

    def dot(x, y):
        return jnp.dot(x, y, preferred_element_type=jnp.float32)

    halves = choice(0, MAIN)[:, 0 : 2 * own_rows]
    pieces = choice(MAIN, REST)

    def stack(begin, step, amount):
        parts = [normed[:, begin + e * step : begin + (e + 1) * step] for e in range(amount)]
        return jnp.concatenate(parts, axis=0)

    def pack(ch):
        packed = dot(halves, stack(ch * CHUNK, HALF, 2))
        blocks[ch, mine_at, :, 0:HALF] = packed.astype(jnp.bfloat16)
        packed = dot(pieces, stack(ch * CHUNK, PIECE, 8))
        blocks[ch, mine_at, :, HALF:WIDE] = packed.astype(jnp.bfloat16)

    sent = [[] for ch in range(chunks)]

    def remote(ch, begin, end, amount, slot, peer):
        return pltpu.make_async_remote_copy(
            src_ref=blocks.at[ch, pl.ds(begin, amount)],
            dst_ref=blocks.at[ch, pl.ds(end, amount)],
            send_sem=send_sem.at[ch, slot],
            recv_sem=recv_sem.at[ch, end],
            device_id={"tensor": peer},
            device_id_type=MESH,
        )

    def send(ch, begin, end, amount, peer):
        remote(ch, begin, end, amount, len(sent[ch]), peer).start()
        sent[ch].append(amount)

    def arrive(ch, begin, amount):
        remote(ch, begin, begin, amount, 0, (me + 1) % n).wait_recv()

    def to_b(ch, begin, amount):
        for j in range(1, nb):
            send(ch, begin, begin, amount, at(0, j, 0))

    def to_c(ch, begin, amount):
        for k in range(1, nc):
            send(ch, begin, begin, amount, at(0, 0, k))

    def along_a(ch):
        for i in range(1, na):
            send(ch, mine_at, mine_at + na - i, 1, at(i, 0, 0))

    def own(ch):
        to_b(ch, mine_at, 1)
        to_c(ch, mine_at, 1)

    def column_on(ch):
        for i in range(1, na):
            arrive(ch, mine_at + i, 1)
        to_b(ch, mine_at + 1, na - 1)
        to_c(ch, mine_at + 1, na - 1)

    early = na // 2

    def across(ch):
        for j in range(1, nb):
            arrive(ch, slot_of(j, 0), 1)
            arrive(ch, slot_of(j, 0) + 1, na - 1)
            to_c(ch, slot_of(j, 0), early)
        for k in range(1, nc):
            arrive(ch, slot_of(0, k), 1)
            arrive(ch, slot_of(0, k) + 1, na - 1)
            to_b(ch, slot_of(0, k) + early, na - early)

    def settle(ch):
        for j in range(1, nb):
            for k in range(1, nc):
                arrive(ch, slot_of(j, k), early)
                arrive(ch, slot_of(j, k) + early, na - early)

    def meta_copy(p):
        return pltpu.make_async_remote_copy(
            src_ref=meta.at[me],
            dst_ref=meta.at[me],
            send_sem=meta_send.at[p],
            recv_sem=meta_recv.at[me],
            device_id={"tensor": (me + p) % n},
            device_id_type=MESH,
        )

    def stat_copy(p):
        return pltpu.make_async_remote_copy(
            src_ref=stats.at[me],
            dst_ref=stats.at[me],
            send_sem=stat_send.at[p],
            recv_sem=stat_recv.at[me],
            device_id={"tensor": (me + p) % n},
            device_id_type=MESH,
        )

    pack(0)
    pl.semaphore_wait(barrier, n - 1)
    along_a(0)
    own(0)
    for ch in range(1, chunks):
        pack(ch)
        along_a(ch)
        own(ch)
        if ch == min(2, chunks - 1):
            column_on(0)
    column_on(1)

    across(0)

    def slot_at(block):
        return block // na * na + (block % na + na - a) % na

    groups = n // GROUP
    size = GROUP * TOK
    in_row = iota((size, size), 0)
    out_col = iota((size, size), 1)
    span = GROUP * MAIN
    source = slot_at((out_col % span) // MAIN) * TOK + out_col // span * MAIN + out_col % MAIN
    main_perm[...] = jnp.where(in_row == source, 1.0, 0.0).astype(jnp.bfloat16)
    tail = cols - n * MAIN
    in_row = iota((size, tail), 0)
    for g in range(groups):
        out_col = iota((size, tail), 1) - g * GROUP * REST
        valid = (out_col >= 0) & (out_col < GROUP * REST)
        out_col = jnp.maximum(out_col, 0)
        for e in range(8):
            source = slot_at(out_col // REST) * TOK + e * REST + out_col % REST
            rest_perm[g * 8 + e] = jnp.where(valid & (in_row == source), 1.0, 0.0).astype(
                jnp.bfloat16
            )

    def turned(x, y):
        return lax.dot_general(
            x, y, (((0,), (0,)), ((), ())), preferred_element_type=jnp.float32
        )

    def unpack(ch):
        span = GROUP * MAIN
        tops = [
            blocks[ch, g * GROUP : (g + 1) * GROUP, :, 0:HALF].reshape(size, HALF)
            for g in range(groups)
        ]
        rests = [
            blocks[ch, g * GROUP : (g + 1) * GROUP, :, HALF:WIDE].reshape(size, PIECE)
            for g in range(groups)
        ]
        for g in range(groups):
            main = turned(tops[g], main_perm[...]).astype(jnp.bfloat16)
            for h in range(2):
                rows[h * HALF : (h + 1) * HALF, g * span : (g + 1) * span] = main[
                    :, h * span : (h + 1) * span
                ]
        for e in range(8):
            rest = sum(turned(rests[g], rest_perm[g * 8 + e]) for g in range(groups))
            rows[e * PIECE : (e + 1) * PIECE, n * MAIN : cols] = rest.astype(jnp.bfloat16)

    padded = scores.shape[0]

    def partial(ch):
        head_copy(ch).wait()
        found = []
        for begin in range(0, vocab, 512):
            amount = min(512, vocab - begin)
            tile = dot(head[ch, begin : begin + amount, :], rows[...])
            if ch > 0:
                tile = tile + scores[begin : begin + amount, :]
            scores[begin : begin + amount, :] = tile
            if ch == chunks - 1:
                peak = jnp.max(tile, axis=0, keepdims=True)
                found.append((peak,) + collect(begin, min(begin + 512, padded), peak))
        return found

    def collect(begin, end, peak):
        gathered = [jnp.zeros((8, cols), jnp.float32)] * 3
        for at_row in range(begin, end, 64):
            tile = scores[at_row : min(at_row + 64, end), :]
            centred = tile - peak
            expo = jnp.exp(centred)
            entry = at_row + iota(tile.shape, 0)
            given = jnp.where(entry == local_ids, tile, 0.0)
            gathered = [
                old + jnp.sum(x.reshape(x.shape[0] // 8, 8, cols), axis=0)
                for old, x in zip(gathered, (expo, expo * centred, given))
            ]
        return tuple(jnp.sum(x, axis=0, keepdims=True) for x in gathered)

    def merge(parts):
        peak = functools.reduce(jnp.maximum, [part[0] for part in parts])
        row_sum = spread = picked = 0.0
        for part in parts:
            shift = part[0] - peak
            factor = jnp.exp(shift)
            row_sum = row_sum + factor * part[1]
            spread = spread + factor * (part[2] + shift * part[1])
            picked = picked + part[3]
        return peak, row_sum, spread, picked

    if padded > vocab:
        scores[vocab:padded, :] = jnp.full((padded - vocab, cols), -1e30, jnp.float32)

    column = iota((1, cols), 1)
    in_main = column < n * MAIN
    owner = jnp.where(in_main, column // MAIN, (column - n * MAIN) // REST)
    rank_at = jnp.where(in_main, column % MAIN, MAIN + (column - n * MAIN) % REST)
    rank_at = jnp.where(owner == mine_at + a, rank_at, -1)
    ids = jnp.zeros((1, cols), jnp.int32)
    places = jnp.zeros((1, cols), jnp.int32)
    for i in range(own_rows):
        ids = jnp.where(rank_at == ranks[i], targets_ref[i], ids)
        places = jnp.where(rank_at == ranks[i], me * own_rows + (i + 1), places)
    meta[me, 0:1, :] = ids
    meta[me, 1:2, :] = places

    @pl.loop(1, n)
    def _(p):
        meta_copy(p).start()

    if chunks > 2:
        column_on(2)
    across(1)
    for ch in range(chunks):
        if ch + 3 < chunks:
            column_on(ch + 3)
        if ch + 2 < chunks:
            across(ch + 2)
        if ch + 1 < chunks:
            settle(ch)
            unpack(ch)
            partial(ch)

    @pl.loop(1, n)
    def _(p):
        other = (me + p) % n
        pltpu.make_async_remote_copy(
            src_ref=meta.at[other],
            dst_ref=meta.at[other],
            send_sem=meta_send.at[p],
            recv_sem=meta_recv.at[other],
            device_id={"tensor": other},
            device_id_type=MESH,
        ).wait_recv()

    ids = sum(meta[s, 0:1, :] for s in range(n))
    places = sum(meta[s, 1:2, :] for s in range(n)) - 1
    local_ids = ids - me * vocab
    local_ids = jnp.where(local_ids < vocab, local_ids, -1)
    settle(chunks - 1)
    unpack(chunks - 1)
    found = partial(chunks - 1)

    peak, row_sum, spread, picked = merge(found)
    stats[me, 0:1, :] = peak
    stats[me, 1:2, :] = row_sum
    stats[me, 2:3, :] = spread
    stats[me, 3:4, :] = picked

    @pl.loop(1, n)
    def _(p):
        stat_copy(p).start()

    tall = iota((own_rows, cols), 0)
    mine = places == me * own_rows + tall
    kept = iota((seqs, 1), 0)
    first = jnp.zeros((seqs, 1), jnp.int32)
    length = jnp.ones((seqs, 1), jnp.int32)
    for k in range(seqs):
        first = jnp.where(kept == k, offsets_ref[k], first)
        length = jnp.where(kept == k, lengths_ref[k], length)
    inside = (places >= first) & (places < first + length)

    @pl.loop(1, n)
    def _(p):
        other = (me + p) % n
        pltpu.make_async_remote_copy(
            src_ref=stats.at[other],
            dst_ref=stats.at[other],
            send_sem=stat_send.at[p],
            recv_sem=stat_recv.at[other],
            device_id={"tensor": other},
            device_id_type=MESH,
        ).wait_recv()

    top, sum_exp, spread, picked = merge(
        [tuple(stats[s, i : i + 1, :] for i in range(4)) for s in range(n)]
    )
    log_total = jnp.log(sum_exp)
    logprob = picked - top - log_total
    entropy = log_total - spread / sum_exp

    def lay(col):
        amount = col.shape[0]
        square = iota((amount, amount), 0) == iota((amount, amount), 1)
        return jnp.sum(jnp.where(square, col, 0.0), axis=0, keepdims=True)

    def total(where, value):
        return jnp.sum(jnp.where(where, value, 0.0), axis=1, keepdims=True)

    result_ref[0:1, 0:own_rows] = lay(total(mine, logprob))
    result_ref[1:2, 0:own_rows] = lay(total(mine, entropy))
    result_ref[2:3, 0:seqs] = lay(total(inside, logprob) / length.astype(jnp.float32))

    for ch in range(chunks):
        for slot, amount in enumerate(sent[ch]):
            remote(ch, 0, 0, amount, slot, (me + 1) % n).wait_send()

    @pl.loop(1, n)
    def _(p):
        meta_copy(p).wait_send()
        stat_copy(p).wait_send()


def local(n, hidden, norm_gain, head_weight, targets, lengths, offsets, loss_mask):
    own_rows, width = hidden.shape
    vocab = head_weight.shape[0]
    seqs = lengths.shape[0]
    chunks = width // CHUNK
    cols = n * MAIN + 128
    hbm = pl.BlockSpec(memory_space=pltpu.HBM)
    vmem = pl.BlockSpec(memory_space=pltpu.VMEM)
    dma = pltpu.SemaphoreType.DMA
    result = pl.pallas_call(
        functools.partial(kernel, n),
        out_shape=jax.ShapeDtypeStruct((8, 128), jnp.float32),
        in_specs=[hbm] * 7,
        out_specs=vmem,
        scratch_shapes=[
            pltpu.SMEM((own_rows,), jnp.int32),
            pltpu.SMEM((seqs,), jnp.int32),
            pltpu.SMEM((seqs,), jnp.int32),
            pltpu.SMEM((own_rows,), jnp.int32),
            pltpu.VMEM((own_rows, width), jnp.bfloat16),
            pltpu.VMEM((width,), jnp.float32),
            pltpu.VMEM((chunks, vocab, CHUNK), jnp.bfloat16),
            pltpu.VMEM((chunks, n, TOK, WIDE), jnp.bfloat16),
            pltpu.VMEM((GROUP * TOK, GROUP * TOK), jnp.bfloat16),
            pltpu.VMEM((n // GROUP * 8, GROUP * TOK, 128), jnp.bfloat16),
            pltpu.VMEM((CHUNK, cols), jnp.bfloat16),
            pltpu.VMEM((-(-vocab // 8) * 8, cols), jnp.float32),
            pltpu.VMEM((n, 2, cols), jnp.int32),
            pltpu.VMEM((n, 4, cols), jnp.float32),
            dma((6,)),
            dma((chunks,)),
            dma((chunks, n)),
            dma((chunks, n)),
            dma((n,)),
            dma((n,)),
            dma((n,)),
            dma((n,)),
        ],
        compiler_params=pltpu.CompilerParams(
            collective_id=0, has_side_effects=True, vmem_limit_bytes=64 * 2**20
        ),
        cost_estimate=pl.CostEstimate(
            flops=2 * vocab * width * n * LIVE,
            bytes_accessed=2 * vocab * width,
            transcendentals=vocab * n * LIVE,
        ),
        name="head_stats",
    )(targets, lengths, offsets, loss_mask, hidden, norm_gain, head_weight)
    sizes = (own_rows, own_rows, seqs)

    def split(packed_ref, *out_refs):
        for i, size in enumerate(sizes):
            out_refs[i][...] = packed_ref[i, 0:size]

    return pl.pallas_call(
        split,
        out_shape=tuple(jax.ShapeDtypeStruct((size,), jnp.float32) for size in sizes),
        in_specs=[vmem],
        out_specs=(vmem, vmem, vmem),
        compiler_params=pltpu.CompilerParams(vmem_limit_bytes=64 * 2**20),
        name="split",
    )(result)


def solution(mesh):
    return jax.shard_map(
        functools.partial(local, mesh.shape["tensor"]),
        mesh=mesh,
        in_specs=(
            P(("dp", "tensor"), None),
            P(),
            P(("dp", "tensor"), None),
            P(("dp", "tensor")),
            P("dp"),
            P("dp"),
            P(("dp", "tensor")),
        ),
        out_specs=(P(("dp", "tensor")), P(("dp", "tensor")), P("dp")),
        check_vma=False,
    )
```
